32 devices in a mesh: node: 8 (over y, x, core), local: 4 (over z).
Axes of the slice: x: 2, y: 2, z: 4, core: 2. Of those that a mesh axis runs over, the one named last changes fastest.
Arguments:
- tokens: bfloat16 [8192, 4096], P(('node', 'local')), may hold values from -6 to 6
- queries: bfloat16 [8192, 4096], P(('node', 'local')), may hold values from -240 to 240
- values: bfloat16 [8192, 512], P(('node', 'local')), may hold values from -6 to 6
- upstream: bfloat16 [8192, 4096], P(('node', 'local')), may hold values from -6 to 6
- key_weight: bfloat16 [4096, 512], P(('node', 'local')), may hold values from -0.09375 to 0.09375
- positions: int32 [8192], P(('node', 'local')), may hold values from 0 to 255, as said below
Outputs:
- grad_tokens: bfloat16 [8192, 4096], P(('node', 'local'))
- grad_weight: float32 [4096, 512], P(('node', 'local'))
The draws below stay inside these ranges and needn't reach their ends.
Inputs may be any that keep to these rules, and one draw needn't show every extreme that they name: positions[i] counts the earlier tokens of token i's document; every block of 256 rows starts a document, and no document crosses such a block.
All inputs are finite; a program needn't handle non-finite values.
Results may differ from the reference program's by a relative error of at most 0.033.
Values may be sent and summed in bfloat16 or wider, within the bound.
No kernel may reach another device: no remote copies, remote signals or barrier semaphores. Data moves between devices by JAX's collectives and lax.ppermute only.
A program may use at most 128 MiB of HBM per device.

```python
import jax
import jax.numpy as jnp
from jax import lax

D = 4096
KEY_VALUE_HEADS = 4
GROUP = 8
HEAD_SIZE = 128
TOK_DEV = 256
HEADS = 32
KEY_WIDTH = 512
TOKENS = 8192


def draw_queries(key, part):
    width = HEADS * HEAD_SIZE
    base = jax.random.normal(key, (TOKENS, width), jnp.float32)
    return jnp.clip(base, -240.0, 240.0).astype(jnp.bfloat16)


def draw_positions(key, part):
    first_key, second_key = jax.random.split(jax.random.fold_in(key, 11))
    place = jnp.arange(TOKENS, dtype=jnp.int32)
    starts = jax.random.randint(first_key, (TOKENS,), 0, 48) == 0
    single = jax.random.randint(second_key, (), 0, TOKENS // TOK_DEV)
    starts = starts & (place // TOK_DEV != single) | (place % TOK_DEV == 0)
    marks = jnp.where(starts, place, 0)
    latest = lax.cummax(marks, axis=0)
    return (place - latest).astype(jnp.int32)


def with_spikes(values, stream_key, source, target, shards_of, factor):
    def block_of(position):
        return (jnp.arange(values.shape[position]) // (values.shape[position] // shards_of)).reshape((-1,) + (1,) * (values.ndim - 1 - position))

    first = jax.random.permutation(stream_key, shards_of)[block_of(target)]
    far = (block_of(target) + shards_of // 2) % shards_of
    return jnp.where((block_of(source) == first) | (block_of(source) == far), factor * values, values)


def block_scale(own_key, shape, pieces, low, top_value):
    def one(dim, shards_of):
        heights = jax.random.uniform(jax.random.fold_in(jax.random.fold_in(own_key, 6), dim), (shards_of,), jnp.float32, low / len(pieces), top_value / len(pieces))
        return jnp.repeat(jnp.exp(heights), shape[dim] // shards_of).reshape((-1,) + (1,) * (len(shape) - dim - 1))

    level = one(*pieces[0])
    for cut in pieces[1:]:
        level = level * one(*cut)
    return level


def noise(stream_key, dims, spread, limit, pieces=(), kind=jnp.bfloat16):
    drawn = jax.random.normal(stream_key, dims, jnp.float32) * spread
    if len(pieces) > 0:
        drawn = block_scale(stream_key, dims, pieces, -0.22, 0.18) * drawn
    return jnp.clip(drawn, min=-limit, max=limit).astype(kind)


def bell_draw_with(own_key, shape, deviation, limit, shards, heavy, held_as=jnp.bfloat16):
    entries = deviation * jax.random.normal(own_key, shape, jnp.float32)
    if shards:
        entries = entries * block_scale(own_key, shape, shards, -0.22, 0.18)
    return jnp.clip(with_spikes(entries, jax.random.fold_in(own_key, 3), *heavy), -limit, limit).astype(held_as)


def setup_inputs(seed: int = 0) -> dict:
    arg_keys = jax.random.split(jax.random.key(seed), 7)
    return {
        "tokens": bell_draw_with(arg_keys[0], (TOKENS, D), 1.0, 6.0, ((0, 32),), (0, 1, 32, 2.75)),
        "queries": draw_queries(jax.random.fold_in(arg_keys[6], 71), 0),
        "values": noise(arg_keys[2], (TOKENS, KEY_WIDTH), 1.0, 6.0, ((0, 32),)),
        "upstream": noise(arg_keys[3], (TOKENS, HEADS * HEAD_SIZE), 1.0, 6.0, ((0, 32),)),
        "key_weight": noise(arg_keys[4], (D, KEY_WIDTH), D ** -0.5, 0.09375, ((0, 32),)),
        "positions": draw_positions(jax.random.fold_in(arg_keys[6], 71), 0),
    }


def angle_tables(positions):
    half = HEAD_SIZE // 2
    freq = jnp.exp(-(jnp.arange(half, dtype=jnp.float32) * 2.0 / HEAD_SIZE) * jnp.log(jnp.float32(1000000.0)))
    angle = positions.astype(jnp.float32)[:, None] * freq[None, :]
    return jnp.cos(angle)[:, None, :], jnp.sin(angle)[:, None, :]


def rotate(raw_keys, cosine, sine_part):
    shaped = raw_keys.reshape(raw_keys.shape[0], KEY_VALUE_HEADS, HEAD_SIZE)
    half = HEAD_SIZE // 2
    first, second = shaped[..., :half], shaped[..., half:]
    joined = jnp.concatenate([first * cosine - second * sine_part, second * cosine + first * sine_part], axis=-1)
    return joined.reshape(raw_keys.shape[0], KEY_VALUE_HEADS * HEAD_SIZE)


def unrotate(grad_rot, cosine, sine_part):
    shaped = grad_rot.reshape(grad_rot.shape[0], KEY_VALUE_HEADS, HEAD_SIZE)
    half = HEAD_SIZE // 2
    first, second = shaped[..., :half], shaped[..., half:]
    joined = jnp.concatenate([first * cosine + second * sine_part, second * cosine - first * sine_part], axis=-1)
    return joined.reshape(grad_rot.shape[0], KEY_VALUE_HEADS * HEAD_SIZE)


def attend_back(queries, keys, values, upstream, positions):
    item_count = queries.shape[0]
    scale = HEAD_SIZE ** -0.5
    qmat = queries.reshape(item_count, KEY_VALUE_HEADS, GROUP, HEAD_SIZE).astype(jnp.float32)
    kmat = keys.reshape(item_count, KEY_VALUE_HEADS, HEAD_SIZE).astype(jnp.float32)
    value_matrix = values.reshape(item_count, KEY_VALUE_HEADS, HEAD_SIZE).astype(jnp.float32)
    upper_matrix = upstream.reshape(item_count, KEY_VALUE_HEADS, GROUP, HEAD_SIZE).astype(jnp.float32)
    scores = jnp.einsum('yxru,oxu->xryo', qmat, kmat) * scale
    place = jnp.arange(item_count, dtype=jnp.int32)
    allowed = (place[None, :] <= place[:, None]) & (place[None, :] >= (place - positions)[:, None])
    scores = jnp.where(allowed, scores, jnp.float32(-1e30))
    top = jnp.max(scores, axis=-1, keepdims=True)
    expo = jnp.exp(scores - top)
    probs = expo / jnp.sum(expo, axis=-1, keepdims=True)
    slope_values = jnp.einsum('yxru,oxu->xryo', upper_matrix, value_matrix)
    inner = jnp.sum(probs * slope_values, axis=-1, keepdims=True)
    dscores = (probs * (slope_values - inner) * scale).astype(jnp.bfloat16)
    grad_rot = jnp.einsum('kgts,tkgd->skd', dscores.astype(jnp.float32), qmat)
    return grad_rot.reshape(item_count, KEY_VALUE_HEADS * HEAD_SIZE)


def reference(tokens, queries, values, upstream, key_weight, positions):
    raw_keys = jnp.dot(tokens, key_weight, preferred_element_type=jnp.float32)
    cosine, sine_part = angle_tables(positions)
    keys = rotate(raw_keys, cosine, sine_part).astype(jnp.bfloat16)
    blocks = TOKENS // TOK_DEV

    def one_block(item):
        qblk, kblk, vblk, ublk, pblk, cblk, sblk = item
        grad_rot = attend_back(qblk, kblk, vblk, ublk, pblk)
        return unrotate(grad_rot, cblk, sblk).astype(jnp.bfloat16)

    items = (queries.reshape(blocks, TOK_DEV, -1), keys.reshape(blocks, TOK_DEV, -1),
             values.reshape(blocks, TOK_DEV, -1), upstream.reshape(blocks, TOK_DEV, -1),
             positions.reshape(blocks, TOK_DEV), cosine.reshape(blocks, TOK_DEV, 1, -1),
             sine_part.reshape(blocks, TOK_DEV, 1, -1))
    grad_keys = lax.map(one_block, items).reshape(TOKENS, KEY_VALUE_HEADS * HEAD_SIZE)
    grad_tokens = lax.dot_general(grad_keys, key_weight, (((1,), (1,)), ((), ())),
                                  preferred_element_type=jnp.float32).astype(jnp.bfloat16)
    grad_weight = lax.dot_general(tokens, grad_keys, (((0,), (0,)), ((), ())),
                                  preferred_element_type=jnp.float32)
    return grad_tokens, grad_weight
```

```python
import functools
import math

import jax
import jax.numpy as jnp
from jax import lax
from jax.experimental import pallas as pl
from jax.experimental.pallas import tpu as pltpu
from jax.sharding import PartitionSpec as P

HEAD_SIZE = 128
PAIRS = 2
BATCH = 4
HBM = pl.BlockSpec(memory_space=pltpu.HBM)
VMEM = pl.BlockSpec(memory_space=pltpu.VMEM)
SMEM = pl.BlockSpec(memory_space=pltpu.SMEM)
LAST_LAST = (((1,), (1,)), ((), ()))
MIB = 1 << 20
CHEAP = pl.CostEstimate(flops=1, bytes_accessed=1, transcendentals=0)
PARAMS = pltpu.CompilerParams(vmem_limit_bytes=12 * MIB)


def angle_tables(positions):
    half = HEAD_SIZE // 2
    freq = jnp.exp(
        -(jnp.arange(half, dtype=jnp.float32) * 2.0 / HEAD_SIZE) * jnp.log(jnp.float32(1000000.0))
    )
    angle = positions.astype(jnp.float32)[:, None] * freq[None, :]
    cosine, sine = jnp.cos(angle), jnp.sin(angle)
    return jnp.concatenate([cosine, cosine], axis=1), jnp.concatenate([-sine, sine], axis=1)


def flip(x, axis, mask, size):
    return lax.ppermute(x, axis, [(i, i ^ mask) for i in range(size)])


def line_kernel(place_ref, *refs):
    shards, out_ref = refs[:-1], refs[-1]
    for k, shard in enumerate(shards):
        out_ref[place_ref[1] ^ k] = shard[...]


def put_in_line(place, shards):
    return pl.pallas_call(
        line_kernel,
        out_shape=jax.ShapeDtypeStruct((len(shards), *shards[0].shape), shards[0].dtype),
        in_specs=[SMEM] + [VMEM] * len(shards),
        out_specs=VMEM,
        compiler_params=PARAMS,
        cost_estimate=CHEAP,
        name="line",
    )(place, *shards)


def turn_kernel(*refs):
    half = len(refs) // 2
    for x_ref, out_ref in zip(refs[:half], refs[half:]):
        for chip in range(x_ref.shape[0]):
            out_ref[chip] = x_ref[chip].T


def turn(*arrays):
    chips, count, block = arrays[0].shape
    return pl.pallas_call(
        turn_kernel,
        out_shape=[jax.ShapeDtypeStruct((chips, block, count), arrays[0].dtype)] * len(arrays),
        in_specs=[VMEM] * len(arrays),
        out_specs=[VMEM] * len(arrays),
        compiler_params=PARAMS,
        cost_estimate=CHEAP,
        name="turn",
    )(*arrays)


def raw_kernel(place_ref, x_ref, *refs):
    pieces, out_ref = refs[:-1], refs[-1]
    chip = place_ref[0] // 2
    total = jnp.zeros(out_ref.shape, jnp.float32)
    for m, piece in enumerate(pieces):
        locs, rows, width = piece.shape
        total += jnp.dot(
            x_ref[chip ^ m], piece[...].reshape(locs * rows, width), preferred_element_type=jnp.float32
        )
    out_ref[...] = total


def raw_terms(place, x, pieces):
    chips, count, block = x.shape
    width = pieces[0].shape[2]
    return pl.pallas_call(
        raw_kernel,
        out_shape=jax.ShapeDtypeStruct((count, width), jnp.float32),
        in_specs=[SMEM] + [VMEM] * (1 + len(pieces)),
        out_specs=VMEM,
        compiler_params=PARAMS,
        cost_estimate=CHEAP,
        name="raw",
    )(place, x, *pieces)


def attend_kernel(pair, heads, group, pos_ref, cos_ref, sin_ref, raw_ref, raw2_ref, q, v, u, gk_ref):
    width = heads * HEAD_SIZE
    count = gk_ref.shape[0]
    block = count // 2
    biases = []
    for part in range(2):
        span = block * (part + 1)
        j = lax.broadcasted_iota(jnp.int32, (span, block), 0)
        i = lax.broadcasted_iota(jnp.int32, (span, block), 1) + part * block
        low = i - pos_ref[:, part * block : (part + 1) * block]
        biases.append(jnp.where((j <= i) & (j >= low), jnp.float32(0.0), jnp.float32(-1e30)))
    raw = raw_ref[...] + raw2_ref[...]
    cosine, sine = cos_ref[...], sin_ref[...]
    scale = HEAD_SIZE ** (-0.5)
    slope = scale * math.log2(math.e)
    for head in range(heads):
        cols = slice(head * HEAD_SIZE, (head + 1) * HEAD_SIZE)
        mine = raw[:, cols]
        keys = (mine * cosine + pltpu.roll(mine, HEAD_SIZE // 2, 1) * sine).astype(jnp.bfloat16)
        vals = v[:, pair * width + head * HEAD_SIZE : pair * width + (head + 1) * HEAD_SIZE]
        totals = []
        for part in range(2):
            span = block * (part + 1)
            lines = slice(part * block, (part + 1) * block)
            bias = jnp.concatenate([biases[part]] * BATCH, axis=1)
            total = jnp.zeros((span, HEAD_SIZE), jnp.float32)
            for g in range(0, group, BATCH):
                starts = [((pair * heads + head) * group + g + t) * HEAD_SIZE for t in range(BATCH)]
                at = [slice(start, start + HEAD_SIZE) for start in starts]
                qs = jnp.concatenate([q[lines, a] for a in at], axis=0)
                us = jnp.concatenate([u[lines, a] for a in at], axis=0)
                scores = lax.dot_general(keys[:span], qs, LAST_LAST, preferred_element_type=jnp.float32) + bias
                slopes = lax.dot_general(vals[:span], us, LAST_LAST, preferred_element_type=jnp.float32)
                top = jnp.max(scores, axis=0, keepdims=True)
                expo = jnp.exp2((scores - top) * slope)
                inv = 1.0 / jnp.sum(expo, axis=0, keepdims=True)
                inner = jnp.sum(expo * slopes, axis=0, keepdims=True) * inv
                dscores = (expo * (slopes - inner) * (inv * scale)).astype(jnp.bfloat16)
                total += jnp.dot(dscores, qs, preferred_element_type=jnp.float32)
            totals.append(total)
        drot = jnp.concatenate([totals[0] + totals[1][:block], totals[1][block:]], axis=0)
        gk_ref[:, cols] = (drot * cosine - pltpu.roll(drot, HEAD_SIZE // 2, 1) * sine).astype(jnp.bfloat16)


def attend(pair, group, pos, cosine, sine, raw, raw2, q, v, u):
    count, width = raw.shape
    q, v, u = (pltpu.with_memory_space_constraint(x, pltpu.VMEM) for x in (q, v, u))
    return pl.pallas_call(
        functools.partial(attend_kernel, pair, width // HEAD_SIZE, group),
        out_shape=jax.ShapeDtypeStruct((count, width), jnp.bfloat16),
        in_specs=[VMEM] * 8,
        out_specs=VMEM,
        compiler_params=PARAMS,
        cost_estimate=CHEAP,
        name="attend",
    )(pos, cosine, sine, raw, raw2, q, v, u)


def terms_kernel(place_ref, own_ref, sib_ref, gk_ref, sib_gk_ref, *outs):
    chip = place_ref[0] // 2
    gk, sib_gk = gk_ref[...], sib_gk_ref[...]

    def term(m, dtype):
        total = jnp.dot(own_ref[chip ^ m], gk, preferred_element_type=jnp.float32)
        total += jnp.dot(sib_ref[chip ^ m], sib_gk, preferred_element_type=jnp.float32)
        return total.reshape(outs[0].shape).astype(dtype)

    for m in list(range(1, len(outs))) + [0]:
        outs[m][...] = term(m, outs[m].dtype)


def terms(locs, place, own, sib, gk, sib_gk):
    chips, block, count = own.shape
    width = gk.shape[1]
    outs = [
        jax.ShapeDtypeStruct((locs, block // locs, width), jnp.bfloat16 if m else jnp.float32) for m in range(chips)
    ]
    return pl.pallas_call(
        terms_kernel,
        out_shape=outs,
        in_specs=[SMEM] + [VMEM] * 4,
        out_specs=[VMEM] * len(outs),
        compiler_params=PARAMS,
        cost_estimate=CHEAP,
        name="terms",
    )(place, own, sib, gk, sib_gk)


def add_kernel(locs, place_ref, *refs):
    parts, keep, sends = refs[:-locs], refs[-locs], refs[len(refs) - locs + 1 :]
    for k in range(locs):
        total = parts[0][place_ref[1] ^ k]
        for part in parts[1:]:
            total += part[place_ref[1] ^ k].astype(jnp.float32)
        if k == 0:
            keep[...] = total
        else:
            sends[k - 1][...] = total.astype(jnp.bfloat16)


def add(locs, place, parts):
    rows, width = parts[0].shape[1:]
    return pl.pallas_call(
        functools.partial(add_kernel, locs),
        out_shape=[jax.ShapeDtypeStruct((rows, width), jnp.float32 if k == 0 else jnp.bfloat16) for k in range(locs)],
        in_specs=[SMEM] + [VMEM] * len(parts),
        out_specs=[VMEM] * locs,
        compiler_params=PARAMS,
        cost_estimate=CHEAP,
        name="add",
    )(place, *parts)


def back_kernel(pairs, parts, place_ref, *refs):
    grads, pieces, outs = [g[...] for g in refs[:pairs]], refs[pairs : len(refs) - parts], refs[len(refs) - parts :]
    chips = len(pieces) // pairs
    for m in range(chips):
        total = None
        for pair in range(pairs):
            piece = pieces[pair * chips + m]
            locs, rows, width = piece.shape
            term = lax.dot_general(
                grads[pair], piece[...].reshape(locs * rows, width), LAST_LAST, preferred_element_type=jnp.float32
            )
            total = term if total is None else total + term
        outs[m * parts // chips][m % (chips // parts)] = total.astype(jnp.bfloat16)


def back(place, gks, pieces, block, parts):
    pairs, chips = len(pieces), len(pieces[0])
    return pl.pallas_call(
        functools.partial(back_kernel, pairs, parts),
        out_shape=[jax.ShapeDtypeStruct((chips // parts, gks[0].shape[0], block), jnp.bfloat16)] * parts,
        in_specs=[SMEM] + [VMEM] * (pairs + pairs * chips),
        out_specs=[VMEM] * parts,
        compiler_params=PARAMS,
        cost_estimate=CHEAP,
        name="back",
    )(place, *gks, *[piece for group in pieces for piece in group])


def columns_of(array, chip, core, block):
    return array.at[:, pl.ds(pl.multiple_of((2 * chip + core) * block, block), block)]


def cut_kernel(place_ref, x_hbm, sib_hbm, own_ref, sib_ref, sems):
    core = place_ref[0] & 1
    copies = []
    for chip in range(own_ref.shape[0]):
        for n, (array, out_ref) in enumerate(((x_hbm, own_ref), (sib_hbm, sib_ref))):
            source = columns_of(array, chip, core, own_ref.shape[2])
            copies.append(pltpu.make_async_copy(source, out_ref.at[chip], sems.at[2 * chip + n]))
    for copy in copies:
        copy.start()
    for copy in copies:
        copy.wait()


def cut(place, x, sib_x, chips, block, core):
    count = x.shape[0]
    if block % 128:
        blocks = [array.reshape(count, chips, 2, block).transpose(2, 1, 0, 3) for array in (x, sib_x)]
        return [lax.dynamic_index_in_dim(array, core, axis=0, keepdims=False) for array in blocks]
    return pl.pallas_call(
        cut_kernel,
        out_shape=[jax.ShapeDtypeStruct((chips, count, block), x.dtype)] * 2,
        in_specs=[SMEM, HBM, HBM],
        out_specs=[VMEM] * 2,
        scratch_shapes=[pltpu.SemaphoreType.DMA((2 * chips,))],
        compiler_params=PARAMS,
        cost_estimate=CHEAP,
        name="cut",
    )(place, pin(x), pin(sib_x))


def join_kernel(place_ref, *refs):
    parts, out_hbm, sems = refs[:-2], refs[-2], refs[-1]
    chip, core = place_ref[0] // 2, place_ref[0] & 1
    block = parts[0].shape[2]
    copies = []
    for n, same in enumerate((parts[:1], parts[1:])):
        m = 0
        for part in same:
            for i in range(part.shape[0]):
                target = columns_of(out_hbm, chip ^ m, core ^ n, block)
                copies.append(pltpu.make_async_copy(part.at[i], target, sems.at[2 * m + n]))
                m += 1
    for copy in copies:
        copy.start()
    for copy in copies:
        copy.wait()


def join(place, own, sib, core):
    (own,) = own
    chips, count, block = own.shape
    if block % 128:
        sib = jnp.concatenate(sib)
        both = jnp.where(core == 0, jnp.stack([own, sib]), jnp.stack([sib, own]))
        both = jnp.take(both, jnp.arange(chips) ^ (place[0] // 2), axis=1)
        return both.transpose(2, 1, 0, 3).reshape(count, 2 * chips * block)
    return pl.pallas_call(
        join_kernel,
        out_shape=jax.ShapeDtypeStruct((count, 2 * chips * block), own.dtype),
        in_specs=[SMEM] + [VMEM] * (1 + len(sib)),
        out_specs=HBM,
        scratch_shapes=[pltpu.SemaphoreType.DMA((2 * chips,))],
        compiler_params=PARAMS,
        cost_estimate=CHEAP,
        name="join",
    )(place, own, *sib)


def pin(x):
    return pltpu.with_memory_space_constraint(x, pltpu.HBM)


def after(x, *others):
    return lax.optimization_barrier((x, *others))[0]


def per_device(tokens, queries, values, upstream, key_weight, positions):
    nodes, locs = lax.axis_size("node"), lax.axis_size("local")
    chips = nodes // 2
    key_width = key_weight.shape[1]
    count, model = tokens.shape
    block = model // nodes
    group = queries.shape[1] // key_width
    width = key_width // PAIRS
    node, local = lax.axis_index("node"), lax.axis_index("local")
    core = node & 1
    place = jnp.stack([node, local]).astype(jnp.int32)

    def swap(x):
        return flip(x, "node", 1, nodes)

    sib_tokens = swap(tokens)
    lines, pieces = [], []
    for pair in range(PAIRS):
        own = after(key_weight, lines[-1]) if pair else key_weight
        own = own[:, pair * width : (pair + 1) * width]
        shards = [own] + [flip(own, "local", k, locs) for k in range(1, locs)]
        if pair:
            shards[0] = after(shards[0], own_x, *pieces[-1][1:])
        lines.append(put_in_line(place, shards))
        pieces.append([lines[-1]] + [flip(lines[-1], "node", 2 * m, nodes) for m in range(1, chips)])
        if not pair:
            own_x, sib_x = cut(place, tokens, after(sib_tokens, lines[0]), chips, block, core)
    own_turned, sib_turned = turn(own_x, sib_x)

    cosine, sine = angle_tables(positions)
    pos = positions.reshape(1, count)

    def raw_of(pair, *others):
        sib, own = (after(x, *others) if others else x for x in (sib_x, own_x))
        return raw_terms(place, own, pieces[pair]), swap(raw_terms(place, sib, pieces[pair]))

    gks, sib_gks, sums = [], [], []
    raw, sib_raw = raw_of(0)
    for pair in range(PAIRS):
        last = pair == PAIRS - 1
        if not last:
            raw = after(raw, *pieces[pair + 1][1:3])
        gk = attend(pair, group, pos, cosine, sine, raw, sib_raw, queries, values, upstream)
        gks.append(gk)
        sib_gks.append(swap(gk))
        if not last:
            raw, sib_raw = raw_of(pair + 1, gk)
            gk = after(gk, raw, sib_raw)
        else:
            gk = after(gk, sums[-1][0])
        outs = list(terms(locs, place, own_turned, sib_turned, gk, sib_gks[-1]))
        parts = outs[:1] + [flip(outs[m], "node", 2 * m, nodes) for m in range(1, chips)]
        sums.append(add(locs, place, parts))
        raw = after(raw, outs[0])

    theirs = [swap(part) for part in back(place, sib_gks, pieces, block, 2)]
    mine = back(place, [after(gks[0], outs[0])] + gks[1:], pieces, block, 1)
    grad_tokens = join(place, mine, theirs, core)
    keeps = []
    for total, *sends in sums:
        got = [flip(part, "local", k + 1, locs) for k, part in enumerate(sends)]
        if keeps:
            total = after(total, grad_tokens)
        for part in got:
            total = total + part.astype(jnp.float32)
        keeps.append(total)
    return grad_tokens, jnp.concatenate(keeps, axis=1)


def solution(mesh):
    split = P(("node", "local"), None)
    return jax.shard_map(
        per_device,
        mesh=mesh,
        in_specs=(split, split, split, split, split, P(("node", "local"))),
        out_specs=(split, split),
        check_vma=False,
    )
```

```python
import functools
import math

import jax
import jax.numpy as jnp
from jax import lax
from jax.experimental import pallas as pl
from jax.experimental.pallas import tpu as pltpu
from jax.sharding import PartitionSpec as P

HEAD_SIZE = 128
PAIRS = 2
BATCH = 4
HBM = pl.BlockSpec(memory_space=pltpu.HBM)
VMEM = pl.BlockSpec(memory_space=pltpu.VMEM)
SMEM = pl.BlockSpec(memory_space=pltpu.SMEM)
LAST_LAST = (((1,), (1,)), ((), ()))
MIB = 1 << 20
CHEAP = pl.CostEstimate(flops=1, bytes_accessed=1, transcendentals=0)
PARAMS = pltpu.CompilerParams(vmem_limit_bytes=12 * MIB)


def angle_tables(positions):
    half = HEAD_SIZE // 2
    freq = jnp.exp(
        -(jnp.arange(half, dtype=jnp.float32) * 2.0 / HEAD_SIZE) * jnp.log(jnp.float32(1000000.0))
    )
    angle = positions.astype(jnp.float32)[:, None] * freq[None, :]
    cosine, sine = jnp.cos(angle), jnp.sin(angle)
    return jnp.concatenate([cosine, cosine], axis=1), jnp.concatenate([-sine, sine], axis=1)


def flip(x, axis, mask, size):
    return lax.ppermute(x, axis, [(i, i ^ mask) for i in range(size)])


def line_kernel(pair, place_ref, *refs):
    shards, out_ref = refs[:-1], refs[-1]
    width = out_ref.shape[2]
    for k, shard in enumerate(shards):
        first = pair * width if shard.shape[1] > width else 0
        out_ref[place_ref[1] ^ k] = shard[:, first : first + width]


def put_in_line(pair, width, place, shards):
    return pl.pallas_call(
        functools.partial(line_kernel, pair),
        out_shape=jax.ShapeDtypeStruct((len(shards), shards[0].shape[0], width), shards[0].dtype),
        in_specs=[SMEM] + [VMEM] * len(shards),
        out_specs=VMEM,
        compiler_params=PARAMS,
        cost_estimate=CHEAP,
        name="line",
    )(place, *shards)


def turn_kernel(*refs):
    half = len(refs) // 2
    for x_ref, out_ref in zip(refs[:half], refs[half:]):
        for chip in range(x_ref.shape[0]):
            out_ref[chip] = x_ref[chip].T


def turn(*arrays):
    chips, count, block = arrays[0].shape
    return pl.pallas_call(
        turn_kernel,
        out_shape=[jax.ShapeDtypeStruct((chips, block, count), arrays[0].dtype)] * len(arrays),
        in_specs=[VMEM] * len(arrays),
        out_specs=[VMEM] * len(arrays),
        compiler_params=PARAMS,
        cost_estimate=CHEAP,
        name="turn",
    )(*arrays)


def raw_kernel(place_ref, x_ref, *refs):
    pieces, outs = refs[: x_ref.shape[0]], refs[x_ref.shape[0] :]
    chip = place_ref[0] // 2
    total = jnp.zeros((x_ref.shape[1], pieces[0].shape[2]), jnp.float32)
    for m, piece in enumerate(pieces):
        locs, rows, width = piece.shape
        total += jnp.dot(
            x_ref[chip ^ m], piece[...].reshape(locs * rows, width), preferred_element_type=jnp.float32
        )
    width = outs[0].shape[1]
    for n, out_ref in enumerate(outs):
        out_ref[...] = total[:, n * width : (n + 1) * width]


def raw_terms(place, x, pieces):
    chips, count, block = x.shape
    width = pieces[0].shape[2]
    return pl.pallas_call(
        raw_kernel,
        out_shape=[jax.ShapeDtypeStruct((count, HEAD_SIZE), jnp.float32)] * (width // HEAD_SIZE),
        in_specs=[SMEM] + [VMEM] * (1 + len(pieces)),
        out_specs=[VMEM] * (width // HEAD_SIZE),
        compiler_params=PARAMS,
        cost_estimate=CHEAP,
        name="raw",
    )(place, x, *pieces)


def attend_kernel(pair, heads, group, pos_ref, cos_ref, sin_ref, *refs):
    raws, sib_raws, (q, v, u, gk_ref) = refs[:heads], refs[heads : 2 * heads], refs[2 * heads :]
    width = heads * HEAD_SIZE
    count = gk_ref.shape[0]
    block = count // 2
    biases = []
    for part in range(2):
        span = block * (part + 1)
        j = lax.broadcasted_iota(jnp.int32, (span, block), 0)
        i = lax.broadcasted_iota(jnp.int32, (span, block), 1) + part * block
        low = i - pos_ref[:, part * block : (part + 1) * block]
        biases.append(jnp.where((j <= i) & (j >= low), jnp.float32(0.0), jnp.float32(-1e30)))
    cosine, sine = cos_ref[...], sin_ref[...]
    scale = HEAD_SIZE ** (-0.5)
    slope = scale * math.log2(math.e)
    for head in range(heads):
        cols = slice(head * HEAD_SIZE, (head + 1) * HEAD_SIZE)
        mine = raws[head][...] + sib_raws[head][...]
        keys = (mine * cosine + pltpu.roll(mine, HEAD_SIZE // 2, 1) * sine).astype(jnp.bfloat16)
        vals = v[:, pair * width + head * HEAD_SIZE : pair * width + (head + 1) * HEAD_SIZE]
        totals = []
        for part in range(2):
            span = block * (part + 1)
            lines = slice(part * block, (part + 1) * block)
            bias = jnp.concatenate([biases[part]] * BATCH, axis=1)
            total = jnp.zeros((span, HEAD_SIZE), jnp.float32)
            for g in range(0, group, BATCH):
                starts = [((pair * heads + head) * group + g + t) * HEAD_SIZE for t in range(BATCH)]
                at = [slice(start, start + HEAD_SIZE) for start in starts]
                qs = jnp.concatenate([q[lines, a] for a in at], axis=0)
                us = jnp.concatenate([u[lines, a] for a in at], axis=0)
                scores = lax.dot_general(keys[:span], qs, LAST_LAST, preferred_element_type=jnp.float32) + bias
                slopes = lax.dot_general(vals[:span], us, LAST_LAST, preferred_element_type=jnp.float32)
                top = jnp.max(scores, axis=0, keepdims=True)
                expo = jnp.exp2((scores - top) * slope)
                inv = 1.0 / jnp.sum(expo, axis=0, keepdims=True)
                inner = jnp.sum(expo * slopes, axis=0, keepdims=True) * inv
                dscores = (expo * (slopes - inner) * (inv * scale)).astype(jnp.bfloat16)
                total += jnp.dot(dscores, qs, preferred_element_type=jnp.float32)
            totals.append(total)
        drot = jnp.concatenate([totals[0] + totals[1][:block], totals[1][block:]], axis=0)
        gk_ref[:, cols] = (drot * cosine - pltpu.roll(drot, HEAD_SIZE // 2, 1) * sine).astype(jnp.bfloat16)


def attend(pair, group, pos, cosine, sine, raw, sib_raw, q, v, u):
    heads, (count, width) = len(raw), raw[0].shape
    q, v, u = (pltpu.with_memory_space_constraint(x, pltpu.VMEM) for x in (q, v, u))
    return pl.pallas_call(
        functools.partial(attend_kernel, pair, heads, group),
        out_shape=jax.ShapeDtypeStruct((count, heads * width), jnp.bfloat16),
        in_specs=[VMEM] * (6 + 2 * heads),
        out_specs=VMEM,
        compiler_params=PARAMS,
        cost_estimate=CHEAP,
        name="attend",
    )(pos, cosine, sine, *raw, *sib_raw, q, v, u)


def terms_kernel(place_ref, own_ref, sib_ref, gk_ref, sib_gk_ref, *outs):
    chip = place_ref[0] // 2
    gk, sib_gk = gk_ref[...], sib_gk_ref[...]

    def term(m, dtype):
        total = jnp.dot(own_ref[chip ^ m], gk, preferred_element_type=jnp.float32)
        total += jnp.dot(sib_ref[chip ^ m], sib_gk, preferred_element_type=jnp.float32)
        return total.reshape(outs[0].shape).astype(dtype)

    for m in list(range(1, len(outs))) + [0]:
        outs[m][...] = term(m, outs[m].dtype)


def terms(locs, place, own, sib, gk, sib_gk):
    chips, block, count = own.shape
    width = gk.shape[1]
    outs = [
        jax.ShapeDtypeStruct((locs, block // locs, width), jnp.bfloat16 if m else jnp.float32) for m in range(chips)
    ]
    return pl.pallas_call(
        terms_kernel,
        out_shape=outs,
        in_specs=[SMEM] + [VMEM] * 4,
        out_specs=[VMEM] * len(outs),
        compiler_params=PARAMS,
        cost_estimate=CHEAP,
        name="terms",
    )(place, own, sib, gk, sib_gk)


def add_kernel(locs, count, place_ref, *refs):
    parts, earlier, outs = refs[:count], refs[count:-locs], refs[-locs:]
    width = outs[0].shape[1]
    for k in range(locs):
        total = parts[0][place_ref[1] ^ k]
        for part in parts[1:]:
            total += part[place_ref[1] ^ k].astype(jnp.float32)
        if k == 1:
            for n, ref in enumerate(earlier):
                outs[k][:, n * width : (n + 1) * width] = ref[...]
            outs[k][:, len(earlier) * width :] = total.astype(jnp.bfloat16)
        else:
            outs[k][...] = total.astype(outs[k].dtype)


def add(locs, place, parts, earlier):
    rows, width = parts[0].shape[1:]
    outs = [jax.ShapeDtypeStruct((rows, width), jnp.bfloat16 if k else jnp.float32) for k in range(locs)]
    outs[1] = jax.ShapeDtypeStruct((rows, (len(earlier) + 1) * width), jnp.bfloat16)
    return pl.pallas_call(
        functools.partial(add_kernel, locs, len(parts)),
        out_shape=outs,
        in_specs=[SMEM] + [VMEM] * (len(parts) + len(earlier)),
        out_specs=[VMEM] * locs,
        compiler_params=PARAMS,
        cost_estimate=CHEAP,
        name="add",
    )(place, *parts, *earlier)


def back_kernel(pairs, parts, place_ref, *refs):
    grads, pieces, outs = [g[...] for g in refs[:pairs]], refs[pairs : len(refs) - parts], refs[len(refs) - parts :]
    chips = len(pieces) // pairs
    for m in range(chips):
        total = None
        for pair in range(pairs):
            piece = pieces[pair * chips + m]
            locs, rows, width = piece.shape
            term = lax.dot_general(
                grads[pair], piece[...].reshape(locs * rows, width), LAST_LAST, preferred_element_type=jnp.float32
            )
            total = term if total is None else total + term
        outs[m * parts // chips][m % (chips // parts)] = total.astype(jnp.bfloat16)


def back(place, gks, pieces, block, parts):
    pairs, chips = len(pieces), len(pieces[0])
    return pl.pallas_call(
        functools.partial(back_kernel, pairs, parts),
        out_shape=[jax.ShapeDtypeStruct((chips // parts, gks[0].shape[0], block), jnp.bfloat16)] * parts,
        in_specs=[SMEM] + [VMEM] * (pairs + pairs * chips),
        out_specs=[VMEM] * parts,
        compiler_params=PARAMS,
        cost_estimate=CHEAP,
        name="back",
    )(place, *gks, *[piece for group in pieces for piece in group])


def columns_of(array, chip, core, block):
    return array.at[:, pl.ds(pl.multiple_of((2 * chip + core) * block, block), block)]


def cut_kernel(place_ref, x_hbm, sib_hbm, own_ref, sib_ref, sems):
    core = place_ref[0] & 1
    copies = []
    for chip in range(own_ref.shape[0]):
        for n, (array, out_ref) in enumerate(((x_hbm, own_ref), (sib_hbm, sib_ref))):
            source = columns_of(array, chip, core, own_ref.shape[2])
            copies.append(pltpu.make_async_copy(source, out_ref.at[chip], sems.at[2 * chip + n]))
    for copy in copies:
        copy.start()
    for copy in copies:
        copy.wait()


def cut(place, x, sib_x, chips, block, core):
    count = x.shape[0]
    if block % 128:
        blocks = [array.reshape(count, chips, 2, block).transpose(2, 1, 0, 3) for array in (x, sib_x)]
        return [lax.dynamic_index_in_dim(array, core, axis=0, keepdims=False) for array in blocks]
    return pl.pallas_call(
        cut_kernel,
        out_shape=[jax.ShapeDtypeStruct((chips, count, block), x.dtype)] * 2,
        in_specs=[SMEM, HBM, pl.BlockSpec(memory_space=pl.ANY)],
        out_specs=[VMEM] * 2,
        scratch_shapes=[pltpu.SemaphoreType.DMA((2 * chips,))],
        compiler_params=PARAMS,
        cost_estimate=CHEAP,
        name="cut",
    )(place, pin(x), sib_x)


def join_kernel(place_ref, *refs):
    parts, out_hbm, sems = refs[:-2], refs[-2], refs[-1]
    chip, core = place_ref[0] // 2, place_ref[0] & 1
    block = parts[0].shape[2]
    copies = []
    for n, same in enumerate((parts[:1], parts[1:])):
        m = 0
        for part in same:
            for i in range(part.shape[0]):
                target = columns_of(out_hbm, chip ^ m, core ^ n, block)
                copies.append(pltpu.make_async_copy(part.at[i], target, sems.at[2 * m + n]))
                m += 1
    for copy in copies:
        copy.start()
    for copy in copies:
        copy.wait()


def join(place, own, sib, core):
    (own,) = own
    chips, count, block = own.shape
    if block % 128:
        sib = jnp.concatenate(sib)
        both = jnp.where(core == 0, jnp.stack([own, sib]), jnp.stack([sib, own]))
        both = jnp.take(both, jnp.arange(chips) ^ (place[0] // 2), axis=1)
        return both.transpose(2, 1, 0, 3).reshape(count, 2 * chips * block)
    return pl.pallas_call(
        join_kernel,
        out_shape=jax.ShapeDtypeStruct((count, 2 * chips * block), own.dtype),
        in_specs=[SMEM] + [VMEM] * (1 + len(sib)),
        out_specs=HBM,
        scratch_shapes=[pltpu.SemaphoreType.DMA((2 * chips,))],
        compiler_params=PARAMS,
        cost_estimate=CHEAP,
        name="join",
    )(place, own, *sib)


def pin(x):
    return pltpu.with_memory_space_constraint(x, pltpu.HBM)


def after(x, *others):
    return lax.optimization_barrier((x, *others))[0]


def per_device(tokens, queries, values, upstream, key_weight, positions):
    nodes, locs = lax.axis_size("node"), lax.axis_size("local")
    chips = nodes // 2
    key_width = key_weight.shape[1]
    count, model = tokens.shape
    block = model // nodes
    group = queries.shape[1] // key_width
    width = key_width // PAIRS
    node, local = lax.axis_index("node"), lax.axis_index("local")
    core = node & 1
    place = jnp.stack([node, local]).astype(jnp.int32)

    def swap(x):
        return flip(x, "node", 1, nodes)

    sib_tokens = swap(tokens)
    lines, pieces = [], []
    beside = flip(key_weight, "local", 1, locs)
    for pair in range(PAIRS):
        own = key_weight[:, pair * width : (pair + 1) * width]
        if pair:
            own = after(own, lines[-1])
        shards = [own, beside] + [flip(own, "local", k, locs) for k in range(2, locs)]
        shards[-1] = after(shards[-1], *((own_x, pieces[-1][-1]) if pair else (sib_tokens,)))
        lines.append(put_in_line(pair, width, place, shards))
        pieces.append([lines[-1]] + [flip(lines[-1], "node", 2 * m, nodes) for m in range(1, chips)])
        if not pair:
            own_x, sib_x = cut(place, tokens, after(sib_tokens, lines[0]), chips, block, core)
    own_turned, sib_turned = turn(own_x, sib_x)

    cosine, sine = angle_tables(positions)
    pos = positions.reshape(1, count)

    def raw_of(pair, *others):
        sib, own = (after(x, *others) if others else x for x in (sib_x, own_x))
        return raw_terms(place, own, pieces[pair]), [swap(part) for part in raw_terms(place, sib, pieces[pair])]

    gks, sib_gks, sums, got = [], [], [], []
    raw, sib_raw = raw_of(0)
    for pair in range(PAIRS):
        gk = attend(pair, group, pos, cosine, sine, raw, sib_raw, queries, values, upstream)
        gks.append(gk)
        sib_gks.append(swap(gk))
        if pair:
            gk = after(gk, sums[-1][0])
        outs = list(terms(locs, place, own_turned, sib_turned, gk, sib_gks[-1]))
        if pair + 1 < PAIRS:
            raw, sib_raw = raw_of(pair + 1, outs[0])
        parts = outs[:1] + [flip(outs[m], "node", 2 * m, nodes) for m in range(1, chips)]
        if pair + 1 == PAIRS:
            theirs, mine = (
                back(place, [after(grads[0], outs[0])] + grads[1:], pieces, block, 1)[0] for grads in (sib_gks, gks)
            )
            parts[0] = after(parts[0], theirs, mine, *got[-1])
        sums.append(add(locs, place, parts, [part[1] for part in sums]))
        got.append([flip(sums[-1][k], "local", k, locs) for k in range(2, locs)])

    beside = flip(sums[-1][1], "local", 1, locs)
    grad_tokens = join(place, [mine], [swap(after(theirs, sums[-1][0]))], core)
    wholes = []
    for pair, parts in enumerate(got):
        whole = after(sums[pair][0], grad_tokens)
        for part in [beside[:, pair * width : (pair + 1) * width]] + parts:
            whole = whole + part.astype(jnp.float32)
        wholes.append(whole)
    return grad_tokens, jnp.concatenate(wholes, axis=1)


def solution(mesh):
    split = P(("node", "local"), None)
    return jax.shard_map(
        per_device,
        mesh=mesh,
        in_specs=(split, split, split, split, split, P(("node", "local"))),
        out_specs=(split, split),
        check_vma=False,
    )
```

```python
import functools
import math

import jax
import jax.numpy as jnp
from jax import lax
from jax.experimental import pallas as pl
from jax.experimental.pallas import tpu as pltpu
from jax.sharding import PartitionSpec as P

HEAD_SIZE = 128
PAIRS = 2
BATCH = 4
HBM = pl.BlockSpec(memory_space=pltpu.HBM)
VMEM = pl.BlockSpec(memory_space=pltpu.VMEM)
SMEM = pl.BlockSpec(memory_space=pltpu.SMEM)
LAST_LAST = (((1,), (1,)), ((), ()))
MIB = 1 << 20
CHEAP = pl.CostEstimate(flops=1, bytes_accessed=1, transcendentals=0)
PARAMS = pltpu.CompilerParams(vmem_limit_bytes=12 * MIB)


def angle_tables(positions):
    half = HEAD_SIZE // 2
    freq = jnp.exp(
        -(jnp.arange(half, dtype=jnp.float32) * 2.0 / HEAD_SIZE) * jnp.log(jnp.float32(1000000.0))
    )
    angle = positions.astype(jnp.float32)[:, None] * freq[None, :]
    cosine, sine = jnp.cos(angle), jnp.sin(angle)
    return jnp.concatenate([cosine, cosine], axis=1), jnp.concatenate([-sine, sine], axis=1)


def flip(x, axis, mask, size):
    return lax.ppermute(x, axis, [(i, i ^ mask) for i in range(size)])


def line_kernel(pair, place_ref, *refs):
    shards, out_ref = refs[:-1], refs[-1]
    width = out_ref.shape[2]
    for k, shard in enumerate(shards):
        first = pair * width if shard.shape[1] > width else 0
        out_ref[place_ref[1] ^ k] = shard[:, first : first + width]


def put_in_line(pair, width, place, shards):
    return pl.pallas_call(
        functools.partial(line_kernel, pair),
        out_shape=jax.ShapeDtypeStruct((len(shards), shards[0].shape[0], width), shards[0].dtype),
        in_specs=[SMEM] + [VMEM] * len(shards),
        out_specs=VMEM,
        compiler_params=PARAMS,
        cost_estimate=CHEAP,
        name="line",
    )(place, *shards)


def turn_kernel(*refs):
    half = len(refs) // 2
    for x_ref, out_ref in zip(refs[:half], refs[half:]):
        for chip in range(x_ref.shape[0]):
            out_ref[chip] = x_ref[chip].T


def turn(*arrays):
    chips, count, block = arrays[0].shape
    return pl.pallas_call(
        turn_kernel,
        out_shape=[jax.ShapeDtypeStruct((chips, block, count), arrays[0].dtype)] * len(arrays),
        in_specs=[VMEM] * len(arrays),
        out_specs=[VMEM] * len(arrays),
        compiler_params=PARAMS,
        cost_estimate=CHEAP,
        name="turn",
    )(*arrays)


def raw_kernel(place_ref, x_ref, *refs):
    pieces, outs = refs[: x_ref.shape[0]], refs[x_ref.shape[0] :]
    chip = place_ref[0] // 2
    total = jnp.zeros((x_ref.shape[1], pieces[0].shape[2]), jnp.float32)
    for m, piece in enumerate(pieces):
        locs, rows, width = piece.shape
        total += jnp.dot(
            x_ref[chip ^ m], piece[...].reshape(locs * rows, width), preferred_element_type=jnp.float32
        )
    width = outs[0].shape[1]
    for n, out_ref in enumerate(outs):
        out_ref[...] = total[:, n * width : (n + 1) * width]


def raw_terms(place, x, pieces):
    chips, count, block = x.shape
    width = pieces[0].shape[2]
    return pl.pallas_call(
        raw_kernel,
        out_shape=[jax.ShapeDtypeStruct((count, HEAD_SIZE), jnp.float32)] * (width // HEAD_SIZE),
        in_specs=[SMEM] + [VMEM] * (1 + len(pieces)),
        out_specs=[VMEM] * (width // HEAD_SIZE),
        compiler_params=PARAMS,
        cost_estimate=CHEAP,
        name="raw",
    )(place, x, *pieces)


def attend_kernel(pair, heads, group, pos_ref, cos_ref, sin_ref, *refs):
    raws, sib_raws, (q, v, u), outs = refs[:heads], refs[heads : 2 * heads], refs[2 * heads : 2 * heads + 3], refs[-heads:]
    width = heads * HEAD_SIZE
    count = outs[0].shape[0]
    block = count // 2
    biases = []
    for part in range(2):
        span = block * (part + 1)
        j = lax.broadcasted_iota(jnp.int32, (span, block), 0)
        i = lax.broadcasted_iota(jnp.int32, (span, block), 1) + part * block
        low = i - pos_ref[:, part * block : (part + 1) * block]
        biases.append(jnp.where((j <= i) & (j >= low), jnp.float32(0.0), jnp.float32(-1e30)))
    cosine, sine = cos_ref[...], sin_ref[...]
    scale = HEAD_SIZE ** (-0.5)
    slope = scale * math.log2(math.e)
    for head in range(heads):
        mine = raws[head][...] + sib_raws[head][...]
        keys = (mine * cosine + pltpu.roll(mine, HEAD_SIZE // 2, 1) * sine).astype(jnp.bfloat16)
        vals = v[:, pair * width + head * HEAD_SIZE : pair * width + (head + 1) * HEAD_SIZE]
        totals = []
        for part in range(2):
            span = block * (part + 1)
            lines = slice(part * block, (part + 1) * block)
            bias = jnp.concatenate([biases[part]] * BATCH, axis=1)
            total = jnp.zeros((span, HEAD_SIZE), jnp.float32)
            for g in range(0, group, BATCH):
                starts = [((pair * heads + head) * group + g + t) * HEAD_SIZE for t in range(BATCH)]
                at = [slice(start, start + HEAD_SIZE) for start in starts]
                qs = jnp.concatenate([q[lines, a] for a in at], axis=0)
                us = jnp.concatenate([u[lines, a] for a in at], axis=0)
                scores = lax.dot_general(keys[:span], qs, LAST_LAST, preferred_element_type=jnp.float32) + bias
                slopes = lax.dot_general(vals[:span], us, LAST_LAST, preferred_element_type=jnp.float32)
                top = jnp.max(scores, axis=0, keepdims=True)
                expo = jnp.exp2((scores - top) * slope)
                inv = 1.0 / jnp.sum(expo, axis=0, keepdims=True)
                inner = jnp.sum(expo * slopes, axis=0, keepdims=True) * inv
                dscores = (expo * (slopes - inner) * (inv * scale)).astype(jnp.bfloat16)
                total += jnp.dot(dscores, qs, preferred_element_type=jnp.float32)
            totals.append(total)
        drot = jnp.concatenate([totals[0] + totals[1][:block], totals[1][block:]], axis=0)
        outs[head][...] = (drot * cosine - pltpu.roll(drot, HEAD_SIZE // 2, 1) * sine).astype(jnp.bfloat16)


def attend(pair, group, pos, cosine, sine, raw, sib_raw, q, v, u):
    heads, (count, width) = len(raw), raw[0].shape
    q, v, u = (pltpu.with_memory_space_constraint(x, pltpu.VMEM) for x in (q, v, u))
    return pl.pallas_call(
        functools.partial(attend_kernel, pair, heads, group),
        out_shape=[jax.ShapeDtypeStruct((count, width), jnp.bfloat16)] * heads,
        in_specs=[VMEM] * (6 + 2 * heads),
        out_specs=[VMEM] * heads,
        compiler_params=PARAMS,
        cost_estimate=CHEAP,
        name="attend",
    )(pos, cosine, sine, *raw, *sib_raw, q, v, u)


def terms_kernel(heads, place_ref, own_ref, sib_ref, *refs):
    outs = refs[2 * heads :]
    chip = place_ref[0] // 2
    gk, sib_gk = (jnp.concatenate([ref[...] for ref in refs[n : n + heads]], axis=1) for n in (0, heads))

    def term(m, dtype):
        total = jnp.dot(own_ref[chip ^ m], gk, preferred_element_type=jnp.float32)
        total += jnp.dot(sib_ref[chip ^ m], sib_gk, preferred_element_type=jnp.float32)
        return total.reshape(outs[0].shape).astype(dtype)

    for m in list(range(1, len(outs))) + [0]:
        outs[m][...] = term(m, outs[m].dtype)


def terms(locs, place, own, sib, gk, sib_gk):
    chips, block, count = own.shape
    heads, width = len(gk), len(gk) * gk[0].shape[1]
    outs = [
        jax.ShapeDtypeStruct((locs, block // locs, width), jnp.bfloat16 if m else jnp.float32) for m in range(chips)
    ]
    return pl.pallas_call(
        functools.partial(terms_kernel, heads),
        out_shape=outs,
        in_specs=[SMEM] + [VMEM] * (2 + 2 * heads),
        out_specs=[VMEM] * len(outs),
        compiler_params=PARAMS,
        cost_estimate=CHEAP,
        name="terms",
    )(place, own, sib, *gk, *sib_gk)


def add_kernel(locs, count, place_ref, *refs):
    parts, earlier, outs = refs[:count], refs[count:-locs], refs[-locs:]
    width = outs[0].shape[1]
    for k in range(locs):
        total = parts[0][place_ref[1] ^ k]
        for part in parts[1:]:
            total += part[place_ref[1] ^ k].astype(jnp.float32)
        if k == 1:
            for n, ref in enumerate(earlier):
                outs[k][:, n * width : (n + 1) * width] = ref[...]
            outs[k][:, len(earlier) * width :] = total.astype(jnp.bfloat16)
        else:
            outs[k][...] = total.astype(outs[k].dtype)


def add(locs, place, parts, earlier):
    rows, width = parts[0].shape[1:]
    outs = [jax.ShapeDtypeStruct((rows, width), jnp.bfloat16 if k else jnp.float32) for k in range(locs)]
    outs[1] = jax.ShapeDtypeStruct((rows, (len(earlier) + 1) * width), jnp.bfloat16)
    return pl.pallas_call(
        functools.partial(add_kernel, locs, len(parts)),
        out_shape=outs,
        in_specs=[SMEM] + [VMEM] * (len(parts) + len(earlier)),
        out_specs=[VMEM] * locs,
        compiler_params=PARAMS,
        cost_estimate=CHEAP,
        name="add",
    )(place, *parts, *earlier)


def back_kernel(pairs, heads, parts, place_ref, *refs):
    pieces, outs = refs[pairs * heads : len(refs) - parts], refs[len(refs) - parts :]
    grads = [
        jnp.concatenate([ref[...] for ref in refs[pair * heads : (pair + 1) * heads]], axis=1) for pair in range(pairs)
    ]
    chips = len(pieces) // pairs
    for m in range(chips):
        total = None
        for pair in range(pairs):
            piece = pieces[pair * chips + m]
            locs, rows, width = piece.shape
            term = lax.dot_general(
                grads[pair], piece[...].reshape(locs * rows, width), LAST_LAST, preferred_element_type=jnp.float32
            )
            total = term if total is None else total + term
        outs[m * parts // chips][m % (chips // parts)] = total.astype(jnp.bfloat16)


def back(place, gks, pieces, block, parts):
    pairs, heads, chips = len(pieces), len(gks[0]), len(pieces[0])
    return pl.pallas_call(
        functools.partial(back_kernel, pairs, heads, parts),
        out_shape=[jax.ShapeDtypeStruct((chips // parts, gks[0][0].shape[0], block), jnp.bfloat16)] * parts,
        in_specs=[SMEM] + [VMEM] * (pairs * heads + pairs * chips),
        out_specs=[VMEM] * parts,
        compiler_params=PARAMS,
        cost_estimate=CHEAP,
        name="back",
    )(place, *[gk for group in gks for gk in group], *[piece for group in pieces for piece in group])


def columns_of(array, chip, core, block):
    return array.at[:, pl.ds(pl.multiple_of((2 * chip + core) * block, block), block)]


def cut_kernel(place_ref, x_hbm, sib_hbm, own_ref, sib_ref, sems):
    core = place_ref[0] & 1
    copies = []
    for chip in range(own_ref.shape[0]):
        for n, (array, out_ref) in enumerate(((x_hbm, own_ref), (sib_hbm, sib_ref))):
            source = columns_of(array, chip, core, own_ref.shape[2])
            copies.append(pltpu.make_async_copy(source, out_ref.at[chip], sems.at[2 * chip + n]))
    for copy in copies:
        copy.start()
    for copy in copies:
        copy.wait()


def cut(place, x, sib_x, chips, block, core):
    count = x.shape[0]
    if block % 128:
        blocks = [array.reshape(count, chips, 2, block).transpose(2, 1, 0, 3) for array in (x, sib_x)]
        return [lax.dynamic_index_in_dim(array, core, axis=0, keepdims=False) for array in blocks]
    return pl.pallas_call(
        cut_kernel,
        out_shape=[jax.ShapeDtypeStruct((chips, count, block), x.dtype)] * 2,
        in_specs=[SMEM, HBM, pl.BlockSpec(memory_space=pl.ANY)],
        out_specs=[VMEM] * 2,
        scratch_shapes=[pltpu.SemaphoreType.DMA((2 * chips,))],
        compiler_params=PARAMS,
        cost_estimate=CHEAP,
        name="cut",
    )(place, pin(x), sib_x)


def join_kernel(place_ref, *refs):
    parts, out_hbm, sems = refs[:-2], refs[-2], refs[-1]
    chip, core = place_ref[0] // 2, place_ref[0] & 1
    block = parts[0].shape[2]
    copies = []
    for n, same in enumerate((parts[:1], parts[1:])):
        m = 0
        for part in same:
            for i in range(part.shape[0]):
                target = columns_of(out_hbm, chip ^ m, core ^ n, block)
                copies.append(pltpu.make_async_copy(part.at[i], target, sems.at[2 * m + n]))
                m += 1
    for copy in copies:
        copy.start()
    for copy in copies:
        copy.wait()


def join(place, own, sib, core):
    (own,) = own
    chips, count, block = own.shape
    if block % 128:
        sib = jnp.concatenate(sib)
        both = jnp.where(core == 0, jnp.stack([own, sib]), jnp.stack([sib, own]))
        both = jnp.take(both, jnp.arange(chips) ^ (place[0] // 2), axis=1)
        return both.transpose(2, 1, 0, 3).reshape(count, 2 * chips * block)
    return pl.pallas_call(
        join_kernel,
        out_shape=jax.ShapeDtypeStruct((count, 2 * chips * block), own.dtype),
        in_specs=[SMEM] + [VMEM] * (1 + len(sib)),
        out_specs=HBM,
        scratch_shapes=[pltpu.SemaphoreType.DMA((2 * chips,))],
        compiler_params=PARAMS,
        cost_estimate=CHEAP,
        name="join",
    )(place, own, *sib)


def pin(x):
    return pltpu.with_memory_space_constraint(x, pltpu.HBM)


def after(x, *others):
    return lax.optimization_barrier((x, *others))[0]


def per_device(tokens, queries, values, upstream, key_weight, positions):
    nodes, locs = lax.axis_size("node"), lax.axis_size("local")
    chips = nodes // 2
    key_width = key_weight.shape[1]
    count, model = tokens.shape
    block = model // nodes
    group = queries.shape[1] // key_width
    width = key_width // PAIRS
    node, local = lax.axis_index("node"), lax.axis_index("local")
    core = node & 1
    place = jnp.stack([node, local]).astype(jnp.int32)

    def swap(x):
        return flip(x, "node", 1, nodes)

    sib_tokens = swap(tokens)
    lines, pieces = [], []
    beside = flip(key_weight, "local", 1, locs)
    for pair in range(PAIRS):
        own = key_weight[:, pair * width : (pair + 1) * width]
        if pair:
            own = after(own, lines[-1])
        shards = [own, beside] + [flip(own, "local", k, locs) for k in range(2, locs)]
        shards[-1] = after(shards[-1], *((own_x, pieces[-1][-1]) if pair else (sib_tokens,)))
        lines.append(put_in_line(pair, width, place, shards))
        pieces.append([lines[-1]] + [flip(lines[-1], "node", 2 * m, nodes) for m in range(1, chips)])
        if not pair:
            own_x, sib_x = cut(place, tokens, after(sib_tokens, lines[0]), chips, block, core)
    own_turned, sib_turned = turn(own_x, sib_x)

    cosine, sine = angle_tables(positions)
    pos = positions.reshape(1, count)

    def raw_of(pair, *others):
        sib, own = (after(x, *others) if others else x for x in (sib_x, own_x))
        return raw_terms(place, own, pieces[pair]), [swap(part) for part in raw_terms(place, sib, pieces[pair])]

    gks, sib_gks, sums, got = [], [], [], []
    raw, sib_raw = raw_of(0)
    for pair in range(PAIRS):
        gks.append(list(attend(pair, group, pos, cosine, sine, raw, sib_raw, queries, values, upstream)))
        sib_gks.append([swap(gk) for gk in gks[-1]])
        outs = list(terms(locs, place, own_turned, sib_turned, gks[-1], sib_gks[-1]))
        if pair + 1 < PAIRS:
            raw, sib_raw = raw_of(pair + 1, outs[0])
        sends = [after(out, *parts[1:]) if pair else out for out in outs]
        parts = outs[:1] + [flip(sends[m], "node", 2 * m, nodes) for m in range(1, chips)]
        if pair + 1 == PAIRS:
            theirs, mine = (
                back(place, [[after(group[0], outs[0])] + group[1:] for group in grads], pieces, block, 1)[0]
                for grads in (sib_gks, gks)
            )
            parts[0] = after(parts[0], theirs, mine, *got[-1])
        sums.append(add(locs, place, parts, [part[1] for part in sums]))
        got.append([flip(sums[-1][k], "local", k, locs) for k in range(2, locs)])

    beside = flip(sums[-1][1], "local", 1, locs)
    grad_tokens = join(place, [mine], [swap(after(theirs, sums[-1][0]))], core)
    wholes = []
    for pair, parts in enumerate(got):
        whole = after(sums[pair][0], grad_tokens)
        for part in [beside[:, pair * width : (pair + 1) * width]] + parts:
            whole = whole + part.astype(jnp.float32)
        wholes.append(whole)
    return grad_tokens, jnp.concatenate(wholes, axis=1)


def solution(mesh):
    split = P(("node", "local"), None)
    return jax.shard_map(
        per_device,
        mesh=mesh,
        in_specs=(split, split, split, split, split, P(("node", "local"))),
        out_specs=(split, split),
        check_vma=False,
    )
```

```python
import functools
import math

import jax
import jax.numpy as jnp
from jax import lax
from jax.experimental import pallas as pl
from jax.experimental.pallas import tpu as pltpu
from jax.sharding import PartitionSpec as P

HEAD_SIZE = 128
PAIRS = 2
BATCH = 4
HBM = pl.BlockSpec(memory_space=pltpu.HBM)
VMEM = pl.BlockSpec(memory_space=pltpu.VMEM)
SMEM = pl.BlockSpec(memory_space=pltpu.SMEM)
LAST_LAST = (((1,), (1,)), ((), ()))
MIB = 1 << 20
CHEAP = pl.CostEstimate(flops=1, bytes_accessed=1, transcendentals=0)
PARAMS = pltpu.CompilerParams(vmem_limit_bytes=12 * MIB)


def angle_tables(positions):
    half = HEAD_SIZE // 2
    freq = jnp.exp(
        -(jnp.arange(half, dtype=jnp.float32) * 2.0 / HEAD_SIZE) * jnp.log(jnp.float32(1000000.0))
    )
    angle = positions.astype(jnp.float32)[:, None] * freq[None, :]
    cosine, sine = jnp.cos(angle), jnp.sin(angle)
    return jnp.concatenate([cosine, cosine], axis=1), jnp.concatenate([-sine, sine], axis=1)


def flip(x, axis, mask, size):
    return lax.ppermute(x, axis, [(i, i ^ mask) for i in range(size)])


def line_kernel(pair, place_ref, *refs):
    shards, out_ref = refs[:-1], refs[-1]
    width = out_ref.shape[2]
    for k, shard in enumerate(shards):
        first = pair * width if shard.shape[1] > width else 0
        out_ref[place_ref[1] ^ k] = shard[:, first : first + width]


def put_in_line(pair, width, place, shards):
    return pl.pallas_call(
        functools.partial(line_kernel, pair),
        out_shape=jax.ShapeDtypeStruct((len(shards), shards[0].shape[0], width), shards[0].dtype),
        in_specs=[SMEM] + [VMEM] * len(shards),
        out_specs=VMEM,
        compiler_params=PARAMS,
        cost_estimate=CHEAP,
        name="line",
    )(place, *shards)


def turn_kernel(*refs):
    half = len(refs) // 2
    for x_ref, out_ref in zip(refs[:half], refs[half:]):
        for chip in range(x_ref.shape[0]):
            out_ref[chip] = x_ref[chip].T


def turn(*arrays):
    chips, count, block = arrays[0].shape
    return pl.pallas_call(
        turn_kernel,
        out_shape=[jax.ShapeDtypeStruct((chips, block, count), arrays[0].dtype)] * len(arrays),
        in_specs=[VMEM] * len(arrays),
        out_specs=[VMEM] * len(arrays),
        compiler_params=PARAMS,
        cost_estimate=CHEAP,
        name="turn",
    )(*arrays)


def raw_kernel(place_ref, x_ref, *refs):
    pieces, outs = refs[: x_ref.shape[0]], refs[x_ref.shape[0] :]
    chip = place_ref[0] // 2
    total = jnp.zeros((x_ref.shape[1], pieces[0].shape[2]), jnp.float32)
    for m, piece in enumerate(pieces):
        locs, rows, width = piece.shape
        total += jnp.dot(
            x_ref[chip ^ m], piece[...].reshape(locs * rows, width), preferred_element_type=jnp.float32
        )
    width = outs[0].shape[1]
    for n, out_ref in enumerate(outs):
        out_ref[...] = total[:, n * width : (n + 1) * width]


def raw_terms(place, x, pieces):
    chips, count, block = x.shape
    width = pieces[0].shape[2]
    return pl.pallas_call(
        raw_kernel,
        out_shape=[jax.ShapeDtypeStruct((count, HEAD_SIZE), jnp.float32)] * (width // HEAD_SIZE),
        in_specs=[SMEM] + [VMEM] * (1 + len(pieces)),
        out_specs=[VMEM] * (width // HEAD_SIZE),
        compiler_params=PARAMS,
        cost_estimate=CHEAP,
        name="raw",
    )(place, x, *pieces)


def attend_kernel(pair, heads, group, pos_ref, cos_ref, sin_ref, *refs):
    raws, sib_raws, (q, v, u), outs = refs[:heads], refs[heads : 2 * heads], refs[2 * heads : 2 * heads + 3], refs[-heads:]
    width = heads * HEAD_SIZE
    count = outs[0].shape[0]
    block = count // 2
    biases = []
    for part in range(2):
        span = block * (part + 1)
        j = lax.broadcasted_iota(jnp.int32, (span, block), 0)
        i = lax.broadcasted_iota(jnp.int32, (span, block), 1) + part * block
        low = i - pos_ref[:, part * block : (part + 1) * block]
        biases.append(jnp.where((j <= i) & (j >= low), jnp.float32(0.0), jnp.float32(-1e30)))
    cosine, sine = cos_ref[...], sin_ref[...]
    scale = HEAD_SIZE ** (-0.5)
    slope = scale * math.log2(math.e)
    for head in range(heads):
        mine = raws[head][...] + sib_raws[head][...]
        keys = (mine * cosine + pltpu.roll(mine, HEAD_SIZE // 2, 1) * sine).astype(jnp.bfloat16)
        vals = v[:, pair * width + head * HEAD_SIZE : pair * width + (head + 1) * HEAD_SIZE]
        totals = []
        for part in range(2):
            span = block * (part + 1)
            lines = slice(part * block, (part + 1) * block)
            bias = jnp.concatenate([biases[part]] * BATCH, axis=1)
            total = jnp.zeros((span, HEAD_SIZE), jnp.float32)
            for g in range(0, group, BATCH):
                starts = [((pair * heads + head) * group + g + t) * HEAD_SIZE for t in range(BATCH)]
                at = [slice(start, start + HEAD_SIZE) for start in starts]
                qs = jnp.concatenate([q[lines, a] for a in at], axis=0)
                us = jnp.concatenate([u[lines, a] for a in at], axis=0)
                scores = lax.dot_general(keys[:span], qs, LAST_LAST, preferred_element_type=jnp.float32) + bias
                slopes = lax.dot_general(vals[:span], us, LAST_LAST, preferred_element_type=jnp.float32)
                top = jnp.max(scores, axis=0, keepdims=True)
                expo = jnp.exp2((scores - top) * slope)
                inv = 1.0 / jnp.sum(expo, axis=0, keepdims=True)
                inner = jnp.sum(expo * slopes, axis=0, keepdims=True) * inv
                dscores = (expo * (slopes - inner) * (inv * scale)).astype(jnp.bfloat16)
                total += jnp.dot(dscores, qs, preferred_element_type=jnp.float32)
            totals.append(total)
        drot = jnp.concatenate([totals[0] + totals[1][:block], totals[1][block:]], axis=0)
        outs[head][...] = (drot * cosine - pltpu.roll(drot, HEAD_SIZE // 2, 1) * sine).astype(jnp.bfloat16)


def attend(pair, group, pos, cosine, sine, raw, sib_raw, q, v, u):
    heads, (count, width) = len(raw), raw[0].shape
    q, v, u = (pltpu.with_memory_space_constraint(x, pltpu.VMEM) for x in (q, v, u))
    return pl.pallas_call(
        functools.partial(attend_kernel, pair, heads, group),
        out_shape=[jax.ShapeDtypeStruct((count, width), jnp.bfloat16)] * heads,
        in_specs=[VMEM] * (6 + 2 * heads),
        out_specs=[VMEM] * heads,
        compiler_params=PARAMS,
        cost_estimate=CHEAP,
        name="attend",
    )(pos, cosine, sine, *raw, *sib_raw, q, v, u)


def terms_kernel(heads, place_ref, own_ref, sib_ref, *refs):
    outs = refs[2 * heads :]
    chip = place_ref[0] // 2
    gk, sib_gk = (jnp.concatenate([ref[...] for ref in refs[n : n + heads]], axis=1) for n in (0, heads))

    def term(m, dtype):
        total = jnp.dot(own_ref[chip ^ m], gk, preferred_element_type=jnp.float32)
        total += jnp.dot(sib_ref[chip ^ m], sib_gk, preferred_element_type=jnp.float32)
        return total.reshape(outs[0].shape).astype(dtype)

    for m in list(range(1, len(outs))) + [0]:
        outs[m][...] = term(m, outs[m].dtype)


def terms(locs, place, own, sib, gk, sib_gk):
    chips, block, count = own.shape
    heads, width = len(gk), len(gk) * gk[0].shape[1]
    outs = [
        jax.ShapeDtypeStruct((locs, block // locs, width), jnp.bfloat16 if m else jnp.float32) for m in range(chips)
    ]
    return pl.pallas_call(
        functools.partial(terms_kernel, heads),
        out_shape=outs,
        in_specs=[SMEM] + [VMEM] * (2 + 2 * heads),
        out_specs=[VMEM] * len(outs),
        compiler_params=PARAMS,
        cost_estimate=CHEAP,
        name="terms",
    )(place, own, sib, *gk, *sib_gk)


def add_kernel(locs, count, place_ref, *refs):
    parts, earlier, outs = refs[:count], refs[count:-locs], refs[-locs:]
    width = outs[0].shape[1]
    for k in range(locs):
        total = parts[0][place_ref[1] ^ k]
        for part in parts[1:]:
            total += part[place_ref[1] ^ k].astype(jnp.float32)
        if k == 1:
            for n, ref in enumerate(earlier):
                outs[k][:, n * width : (n + 1) * width] = ref[...]
            outs[k][:, len(earlier) * width :] = total.astype(jnp.bfloat16)
        else:
            outs[k][...] = total.astype(outs[k].dtype)


def add(locs, place, parts, earlier):
    rows, width = parts[0].shape[1:]
    outs = [jax.ShapeDtypeStruct((rows, width), jnp.bfloat16 if k else jnp.float32) for k in range(locs)]
    outs[1] = jax.ShapeDtypeStruct((rows, (len(earlier) + 1) * width), jnp.bfloat16)
    return pl.pallas_call(
        functools.partial(add_kernel, locs, len(parts)),
        out_shape=outs,
        in_specs=[SMEM] + [VMEM] * (len(parts) + len(earlier)),
        out_specs=[VMEM] * locs,
        compiler_params=PARAMS,
        cost_estimate=CHEAP,
        name="add",
    )(place, *parts, *earlier)


def back_kernel(pairs, heads, parts, place_ref, *refs):
    pieces, outs = refs[pairs * heads : len(refs) - parts], refs[len(refs) - parts :]
    grads = [
        jnp.concatenate([ref[...] for ref in refs[pair * heads : (pair + 1) * heads]], axis=1) for pair in range(pairs)
    ]
    chips = len(pieces) // pairs
    for m in range(chips):
        total = None
        for pair in range(pairs):
            piece = pieces[pair * chips + m]
            locs, rows, width = piece.shape
            term = lax.dot_general(
                grads[pair], piece[...].reshape(locs * rows, width), LAST_LAST, preferred_element_type=jnp.float32
            )
            total = term if total is None else total + term
        outs[m * parts // chips][m % (chips // parts)] = total.astype(jnp.bfloat16)


def back(place, gks, pieces, block, parts):
    pairs, heads, chips = len(pieces), len(gks[0]), len(pieces[0])
    return pl.pallas_call(
        functools.partial(back_kernel, pairs, heads, parts),
        out_shape=[jax.ShapeDtypeStruct((chips // parts, gks[0][0].shape[0], block), jnp.bfloat16)] * parts,
        in_specs=[SMEM] + [VMEM] * (pairs * heads + pairs * chips),
        out_specs=[VMEM] * parts,
        compiler_params=PARAMS,
        cost_estimate=CHEAP,
        name="back",
    )(place, *[gk for group in gks for gk in group], *[piece for group in pieces for piece in group])


def columns_of(array, chip, core, block):
    return array.at[:, pl.ds(pl.multiple_of((2 * chip + core) * block, block), block)]


def cut_kernel(place_ref, x_hbm, sib_hbm, own_ref, sib_ref, sems):
    core = place_ref[0] & 1
    copies = []
    for chip in range(own_ref.shape[0]):
        for n, (array, out_ref) in enumerate(((x_hbm, own_ref), (sib_hbm, sib_ref))):
            source = columns_of(array, chip, core, own_ref.shape[2])
            copies.append(pltpu.make_async_copy(source, out_ref.at[chip], sems.at[2 * chip + n]))
    for copy in copies:
        copy.start()
    for copy in copies:
        copy.wait()


def cut(place, x, sib_x, chips, block, core):
    count = x.shape[0]
    if block % 128:
        blocks = [array.reshape(count, chips, 2, block).transpose(2, 1, 0, 3) for array in (x, sib_x)]
        return [lax.dynamic_index_in_dim(array, core, axis=0, keepdims=False) for array in blocks]
    return pl.pallas_call(
        cut_kernel,
        out_shape=[jax.ShapeDtypeStruct((chips, count, block), x.dtype)] * 2,
        in_specs=[SMEM, HBM, pl.BlockSpec(memory_space=pl.ANY)],
        out_specs=[VMEM] * 2,
        scratch_shapes=[pltpu.SemaphoreType.DMA((2 * chips,))],
        compiler_params=PARAMS,
        cost_estimate=CHEAP,
        name="cut",
    )(place, pin(x), sib_x)


def join_kernel(place_ref, *refs):
    parts, out_hbm, sems = refs[:-2], refs[-2], refs[-1]
    chip, core = place_ref[0] // 2, place_ref[0] & 1
    block = parts[0].shape[2]
    copies = []
    for n, same in enumerate((parts[:1], parts[1:])):
        m = 0
        for part in same:
            for i in range(part.shape[0]):
                target = columns_of(out_hbm, chip ^ m, core ^ n, block)
                copies.append(pltpu.make_async_copy(part.at[i], target, sems.at[2 * m + n]))
                m += 1
    for copy in copies:
        copy.start()
    for copy in copies:
        copy.wait()


def join(place, own, sib, core):
    (own,) = own
    chips, count, block = own.shape
    if block % 128:
        sib = jnp.concatenate(sib)
        both = jnp.where(core == 0, jnp.stack([own, sib]), jnp.stack([sib, own]))
        both = jnp.take(both, jnp.arange(chips) ^ (place[0] // 2), axis=1)
        return both.transpose(2, 1, 0, 3).reshape(count, 2 * chips * block)
    return pl.pallas_call(
        join_kernel,
        out_shape=jax.ShapeDtypeStruct((count, 2 * chips * block), own.dtype),
        in_specs=[SMEM] + [VMEM] * (1 + len(sib)),
        out_specs=HBM,
        scratch_shapes=[pltpu.SemaphoreType.DMA((2 * chips,))],
        compiler_params=PARAMS,
        cost_estimate=CHEAP,
        name="join",
    )(place, own, *sib)


def pin(x):
    return pltpu.with_memory_space_constraint(x, pltpu.HBM)


def after(x, *others):
    return lax.optimization_barrier((x, *others))[0]


def per_device(tokens, queries, values, upstream, key_weight, positions):
    nodes, locs = lax.axis_size("node"), lax.axis_size("local")
    chips = nodes // 2
    key_width = key_weight.shape[1]
    count, model = tokens.shape
    block = model // nodes
    group = queries.shape[1] // key_width
    width = key_width // PAIRS
    node, local = lax.axis_index("node"), lax.axis_index("local")
    core = node & 1
    place = jnp.stack([node, local]).astype(jnp.int32)

    def swap(x):
        return flip(x, "node", 1, nodes)

    sib_tokens = swap(tokens)
    lines, pieces = [], []
    beside = flip(key_weight, "local", 1, locs)
    for pair in range(PAIRS):
        own = key_weight[:, pair * width : (pair + 1) * width]
        if pair:
            own = after(own, lines[-1])
        shards = [own, beside] + [flip(own, "local", k, locs) for k in range(2, locs)]
        shards[-1] = after(shards[-1], *((own_x, pieces[-1][-1]) if pair else (sib_tokens,)))
        lines.append(put_in_line(pair, width, place, shards))
        pieces.append([lines[-1]] + [flip(lines[-1], "node", 2 * m, nodes) for m in range(1, chips)])
        if not pair:
            own_x, sib_x = cut(place, tokens, after(sib_tokens, lines[0]), chips, block, core)
    own_turned, sib_turned = turn(own_x, sib_x)

    cosine, sine = angle_tables(positions)
    pos = positions.reshape(1, count)

    def raw_of(pair, *others):
        sib, own = (after(x, *others) if others else x for x in (sib_x, own_x))
        return raw_terms(place, own, pieces[pair]), [swap(part) for part in raw_terms(place, sib, pieces[pair])]

    gks, sib_gks, sums, got = [], [], [], []
    raw, sib_raw = raw_of(0)
    for pair in range(PAIRS):
        gks.append(list(attend(pair, group, pos, cosine, sine, raw, sib_raw, queries, values, upstream)))
        sib_gks.append([swap(gk) for gk in gks[-1]])
        outs = list(terms(locs, place, own_turned, sib_turned, gks[-1], sib_gks[-1]))
        if pair + 1 < PAIRS:
            raw, sib_raw = raw_of(pair + 1, outs[0])
        sends = [after(out, *parts[1:]) if pair and m == chips - 1 else out for m, out in enumerate(outs)]
        parts = outs[:1] + [flip(sends[m], "node", 2 * m, nodes) for m in range(1, chips)]
        if pair + 1 == PAIRS:
            theirs, mine = (
                back(place, [[after(group[0], outs[0])] + group[1:] for group in grads], pieces, block, 1)[0]
                for grads in (sib_gks, gks)
            )
            parts[0] = after(parts[0], theirs, mine, *got[-1])
        sums.append(add(locs, place, parts, [part[1] for part in sums]))
        got.append([flip(sums[-1][k], "local", k, locs) for k in range(2, locs)])

    beside = flip(sums[-1][1], "local", 1, locs)
    grad_tokens = join(place, [mine], [swap(after(theirs, sums[-1][0]))], core)
    wholes = []
    for pair, parts in enumerate(got):
        whole = after(sums[pair][0], grad_tokens)
        for part in [beside[:, pair * width : (pair + 1) * width]] + parts:
            whole = whole + part.astype(jnp.float32)
        wholes.append(whole)
    return grad_tokens, jnp.concatenate(wholes, axis=1)


def solution(mesh):
    split = P(("node", "local"), None)
    return jax.shard_map(
        per_device,
        mesh=mesh,
        in_specs=(split, split, split, split, split, P(("node", "local"))),
        out_specs=(split, split),
        check_vma=False,
    )
```

```python
import functools
import math

import jax
import jax.numpy as jnp
from jax import lax
from jax.experimental import pallas as pl
from jax.experimental.pallas import tpu as pltpu
from jax.sharding import PartitionSpec as P

HEAD_SIZE = 128
PAIRS = 2
BATCH = 4
HBM = pl.BlockSpec(memory_space=pltpu.HBM)
VMEM = pl.BlockSpec(memory_space=pltpu.VMEM)
SMEM = pl.BlockSpec(memory_space=pltpu.SMEM)
LAST_LAST = (((1,), (1,)), ((), ()))
MIB = 1 << 20
CHEAP = pl.CostEstimate(flops=1, bytes_accessed=1, transcendentals=0)
PARAMS = pltpu.CompilerParams(vmem_limit_bytes=12 * MIB)


def angle_tables(positions):
    half = HEAD_SIZE // 2
    freq = jnp.exp(
        -(jnp.arange(half, dtype=jnp.float32) * 2.0 / HEAD_SIZE) * jnp.log(jnp.float32(1000000.0))
    )
    angle = positions.astype(jnp.float32)[:, None] * freq[None, :]
    cosine, sine = jnp.cos(angle), jnp.sin(angle)
    return jnp.concatenate([cosine, cosine], axis=1), jnp.concatenate([-sine, sine], axis=1)


def flip(x, axis, mask, size):
    return lax.ppermute(x, axis, [(i, i ^ mask) for i in range(size)])


def line_kernel(pair, place_ref, *refs):
    shards, out_ref = refs[:-1], refs[-1]
    width = out_ref.shape[2]
    for k, shard in enumerate(shards):
        first = pair * width if shard.shape[1] > width else 0
        out_ref[place_ref[1] ^ k] = shard[:, first : first + width]


def put_in_line(pair, width, place, shards):
    return pl.pallas_call(
        functools.partial(line_kernel, pair),
        out_shape=jax.ShapeDtypeStruct((len(shards), shards[0].shape[0], width), shards[0].dtype),
        in_specs=[SMEM] + [VMEM] * len(shards),
        out_specs=VMEM,
        compiler_params=PARAMS,
        cost_estimate=CHEAP,
        name="line",
    )(place, *shards)


def turn_kernel(*refs):
    half = len(refs) // 2
    for x_ref, out_ref in zip(refs[:half], refs[half:]):
        for chip in range(x_ref.shape[0]):
            out_ref[chip] = x_ref[chip].T


def turn(*arrays):
    chips, count, block = arrays[0].shape
    return pl.pallas_call(
        turn_kernel,
        out_shape=[jax.ShapeDtypeStruct((chips, block, count), arrays[0].dtype)] * len(arrays),
        in_specs=[VMEM] * len(arrays),
        out_specs=[VMEM] * len(arrays),
        compiler_params=PARAMS,
        cost_estimate=CHEAP,
        name="turn",
    )(*arrays)


def raw_kernel(place_ref, x_ref, *refs):
    pieces, outs = refs[: x_ref.shape[0]], refs[x_ref.shape[0] :]
    chip = place_ref[0] // 2
    total = jnp.zeros((x_ref.shape[1], pieces[0].shape[2]), jnp.float32)
    for m, piece in enumerate(pieces):
        locs, rows, width = piece.shape
        total += jnp.dot(
            x_ref[chip ^ m], piece[...].reshape(locs * rows, width), preferred_element_type=jnp.float32
        )
    width = outs[0].shape[1]
    for n, out_ref in enumerate(outs):
        out_ref[...] = total[:, n * width : (n + 1) * width]


def raw_terms(place, x, pieces):
    chips, count, block = x.shape
    width = pieces[0].shape[2]
    return pl.pallas_call(
        raw_kernel,
        out_shape=[jax.ShapeDtypeStruct((count, HEAD_SIZE), jnp.float32)] * (width // HEAD_SIZE),
        in_specs=[SMEM] + [VMEM] * (1 + len(pieces)),
        out_specs=[VMEM] * (width // HEAD_SIZE),
        compiler_params=PARAMS,
        cost_estimate=CHEAP,
        name="raw",
    )(place, x, *pieces)


def attend_kernel(pair, heads, group, pos_ref, cos_ref, sin_ref, *refs):
    raws, sib_raws, (q, v, u), outs = refs[:heads], refs[heads : 2 * heads], refs[2 * heads : 2 * heads + 3], refs[-heads:]
    width = heads * HEAD_SIZE
    count = outs[0].shape[0]
    block = count // 2
    biases = []
    for part in range(2):
        span = block * (part + 1)
        j = lax.broadcasted_iota(jnp.int32, (span, block), 0)
        i = lax.broadcasted_iota(jnp.int32, (span, block), 1) + part * block
        low = i - pos_ref[:, part * block : (part + 1) * block]
        biases.append(jnp.where((j <= i) & (j >= low), jnp.float32(0.0), jnp.float32(-1e30)))
    cosine, sine = cos_ref[...], sin_ref[...]
    scale = HEAD_SIZE ** (-0.5)
    slope = scale * math.log2(math.e)
    for head in range(heads):
        mine = raws[head][...] + sib_raws[head][...]
        keys = (mine * cosine + pltpu.roll(mine, HEAD_SIZE // 2, 1) * sine).astype(jnp.bfloat16)
        vals = v[:, pair * width + head * HEAD_SIZE : pair * width + (head + 1) * HEAD_SIZE]
        totals = []
        for part in range(2):
            span = block * (part + 1)
            lines = slice(part * block, (part + 1) * block)
            bias = jnp.concatenate([biases[part]] * BATCH, axis=1)
            total = jnp.zeros((span, HEAD_SIZE), jnp.float32)
            for g in range(0, group, BATCH):
                starts = [((pair * heads + head) * group + g + t) * HEAD_SIZE for t in range(BATCH)]
                at = [slice(start, start + HEAD_SIZE) for start in starts]
                qs = jnp.concatenate([q[lines, a] for a in at], axis=0)
                us = jnp.concatenate([u[lines, a] for a in at], axis=0)
                scores = lax.dot_general(keys[:span], qs, LAST_LAST, preferred_element_type=jnp.float32) + bias
                slopes = lax.dot_general(vals[:span], us, LAST_LAST, preferred_element_type=jnp.float32)
                top = jnp.max(scores, axis=0, keepdims=True)
                expo = jnp.exp2((scores - top) * slope)
                inv = 1.0 / jnp.sum(expo, axis=0, keepdims=True)
                inner = jnp.sum(expo * slopes, axis=0, keepdims=True) * inv
                dscores = (expo * (slopes - inner) * (inv * scale)).astype(jnp.bfloat16)
                total += jnp.dot(dscores, qs, preferred_element_type=jnp.float32)
            totals.append(total)
        drot = jnp.concatenate([totals[0] + totals[1][:block], totals[1][block:]], axis=0)
        outs[head][...] = (drot * cosine - pltpu.roll(drot, HEAD_SIZE // 2, 1) * sine).astype(jnp.bfloat16)


def attend(pair, group, pos, cosine, sine, raw, sib_raw, q, v, u):
    heads, (count, width) = len(raw), raw[0].shape
    q, v, u = (pltpu.with_memory_space_constraint(x, pltpu.VMEM) for x in (q, v, u))
    return pl.pallas_call(
        functools.partial(attend_kernel, pair, heads, group),
        out_shape=[jax.ShapeDtypeStruct((count, width), jnp.bfloat16)] * heads,
        in_specs=[VMEM] * (6 + 2 * heads),
        out_specs=[VMEM] * heads,
        compiler_params=PARAMS,
        cost_estimate=CHEAP,
        name="attend",
    )(pos, cosine, sine, *raw, *sib_raw, q, v, u)


def terms_kernel(heads, place_ref, own_ref, sib_ref, *refs):
    outs = refs[2 * heads :]
    chip = place_ref[0] // 2
    gk, sib_gk = (jnp.concatenate([ref[...] for ref in refs[n : n + heads]], axis=1) for n in (0, heads))

    def term(m, dtype):
        total = jnp.dot(own_ref[chip ^ m], gk, preferred_element_type=jnp.float32)
        total += jnp.dot(sib_ref[chip ^ m], sib_gk, preferred_element_type=jnp.float32)
        return total.reshape(outs[0].shape).astype(dtype)

    for m in list(range(1, len(outs))) + [0]:
        outs[m][...] = term(m, outs[m].dtype)


def terms(locs, place, own, sib, gk, sib_gk):
    chips, block, count = own.shape
    heads, width = len(gk), len(gk) * gk[0].shape[1]
    outs = [
        jax.ShapeDtypeStruct((locs, block // locs, width), jnp.bfloat16 if m else jnp.float32) for m in range(chips)
    ]
    return pl.pallas_call(
        functools.partial(terms_kernel, heads),
        out_shape=outs,
        in_specs=[SMEM] + [VMEM] * (2 + 2 * heads),
        out_specs=[VMEM] * len(outs),
        compiler_params=PARAMS,
        cost_estimate=CHEAP,
        name="terms",
    )(place, own, sib, *gk, *sib_gk)


def add_kernel(locs, count, place_ref, *refs):
    parts, earlier, outs = refs[:count], refs[count:-locs], refs[-locs:]
    width = outs[0].shape[1]
    for k in range(locs):
        total = parts[0][place_ref[1] ^ k]
        for part in parts[1:]:
            total += part[place_ref[1] ^ k].astype(jnp.float32)
        if k == 1:
            for n, ref in enumerate(earlier):
                outs[k][:, n * width : (n + 1) * width] = ref[...]
            outs[k][:, len(earlier) * width :] = total.astype(jnp.bfloat16)
        else:
            outs[k][...] = total.astype(outs[k].dtype)


def add(locs, place, parts, earlier):
    rows, width = parts[0].shape[1:]
    outs = [jax.ShapeDtypeStruct((rows, width), jnp.bfloat16 if k else jnp.float32) for k in range(locs)]
    outs[1] = jax.ShapeDtypeStruct((rows, (len(earlier) + 1) * width), jnp.bfloat16)
    return pl.pallas_call(
        functools.partial(add_kernel, locs, len(parts)),
        out_shape=outs,
        in_specs=[SMEM] + [VMEM] * (len(parts) + len(earlier)),
        out_specs=[VMEM] * locs,
        compiler_params=PARAMS,
        cost_estimate=CHEAP,
        name="add",
    )(place, *parts, *earlier)


def back_kernel(pairs, heads, parts, place_ref, *refs):
    pieces, outs = refs[pairs * heads : len(refs) - parts], refs[len(refs) - parts :]
    grads = [
        jnp.concatenate([ref[...] for ref in refs[pair * heads : (pair + 1) * heads]], axis=1) for pair in range(pairs)
    ]
    chips = len(pieces) // pairs
    for m in range(chips):
        total = None
        for pair in range(pairs):
            piece = pieces[pair * chips + m]
            locs, rows, width = piece.shape
            term = lax.dot_general(
                grads[pair], piece[...].reshape(locs * rows, width), LAST_LAST, preferred_element_type=jnp.float32
            )
            total = term if total is None else total + term
        outs[m * parts // chips][m % (chips // parts)] = total.astype(jnp.bfloat16)


def back(place, gks, pieces, block, parts):
    pairs, heads, chips = len(pieces), len(gks[0]), len(pieces[0])
    return pl.pallas_call(
        functools.partial(back_kernel, pairs, heads, parts),
        out_shape=[jax.ShapeDtypeStruct((chips // parts, gks[0][0].shape[0], block), jnp.bfloat16)] * parts,
        in_specs=[SMEM] + [VMEM] * (pairs * heads + pairs * chips),
        out_specs=[VMEM] * parts,
        compiler_params=PARAMS,
        cost_estimate=CHEAP,
        name="back",
    )(place, *[gk for group in gks for gk in group], *[piece for group in pieces for piece in group])


def columns_of(array, chip, core, block):
    return array.at[:, pl.ds(pl.multiple_of((2 * chip + core) * block, block), block)]


def cut_kernel(place_ref, x_hbm, sib_hbm, own_ref, sib_ref, sems):
    core = place_ref[0] & 1
    copies = []
    for chip in range(own_ref.shape[0]):
        for n, (array, out_ref) in enumerate(((x_hbm, own_ref), (sib_hbm, sib_ref))):
            source = columns_of(array, chip, core, own_ref.shape[2])
            copies.append(pltpu.make_async_copy(source, out_ref.at[chip], sems.at[2 * chip + n]))
    for copy in copies:
        copy.start()
    for copy in copies:
        copy.wait()


def cut(place, x, sib_x, chips, block, core):
    count = x.shape[0]
    if block % 128:
        blocks = [array.reshape(count, chips, 2, block).transpose(2, 1, 0, 3) for array in (x, sib_x)]
        return [lax.dynamic_index_in_dim(array, core, axis=0, keepdims=False) for array in blocks]
    return pl.pallas_call(
        cut_kernel,
        out_shape=[jax.ShapeDtypeStruct((chips, count, block), x.dtype)] * 2,
        in_specs=[SMEM, HBM, pl.BlockSpec(memory_space=pl.ANY)],
        out_specs=[VMEM] * 2,
        scratch_shapes=[pltpu.SemaphoreType.DMA((2 * chips,))],
        compiler_params=PARAMS,
        cost_estimate=CHEAP,
        name="cut",
    )(place, pin(x), sib_x)


def join_kernel(place_ref, *refs):
    parts, out_hbm, sems = refs[:-2], refs[-2], refs[-1]
    chip, core = place_ref[0] // 2, place_ref[0] & 1
    block = parts[0].shape[2]
    copies = []
    for n, same in enumerate((parts[:1], parts[1:])):
        m = 0
        for part in same:
            for i in range(part.shape[0]):
                target = columns_of(out_hbm, chip ^ m, core ^ n, block)
                copies.append(pltpu.make_async_copy(part.at[i], target, sems.at[2 * m + n]))
                m += 1
    for copy in copies:
        copy.start()
    for copy in copies:
        copy.wait()


def join(place, own, sib, core):
    (own,) = own
    chips, count, block = own.shape
    if block % 128:
        sib = jnp.concatenate(sib)
        both = jnp.where(core == 0, jnp.stack([own, sib]), jnp.stack([sib, own]))
        both = jnp.take(both, jnp.arange(chips) ^ (place[0] // 2), axis=1)
        return both.transpose(2, 1, 0, 3).reshape(count, 2 * chips * block)
    return pl.pallas_call(
        join_kernel,
        out_shape=jax.ShapeDtypeStruct((count, 2 * chips * block), own.dtype),
        in_specs=[SMEM] + [VMEM] * (1 + len(sib)),
        out_specs=HBM,
        scratch_shapes=[pltpu.SemaphoreType.DMA((2 * chips,))],
        compiler_params=PARAMS,
        cost_estimate=CHEAP,
        name="join",
    )(place, own, *sib)


def pin(x):
    return pltpu.with_memory_space_constraint(x, pltpu.HBM)


def after(x, *others):
    return lax.optimization_barrier((x, *others))[0]


def per_device(tokens, queries, values, upstream, key_weight, positions):
    nodes, locs = lax.axis_size("node"), lax.axis_size("local")
    chips = nodes // 2
    key_width = key_weight.shape[1]
    count, model = tokens.shape
    block = model // nodes
    group = queries.shape[1] // key_width
    width = key_width // PAIRS
    node, local = lax.axis_index("node"), lax.axis_index("local")
    core = node & 1
    place = jnp.stack([node, local]).astype(jnp.int32)

    def swap(x):
        return flip(x, "node", 1, nodes)

    sib_tokens = swap(tokens)
    cosine, sine = angle_tables(positions)
    pos = positions.reshape(1, count)
    lines, pieces = [], []
    beside = flip(key_weight, "local", 1, locs)
    for pair in range(PAIRS):
        own = key_weight[:, pair * width : (pair + 1) * width]
        if pair:
            own = after(own, lines[-1])
        shards = [own, beside] + [flip(own, "local", k, locs) for k in range(2, locs)]
        shards[-1] = after(shards[-1], *((own_x, pieces[-1][-1]) if pair else (sib_tokens, cosine, sine)))
        lines.append(put_in_line(pair, width, place, shards))
        sends = [after(lines[-1], *pieces[-1][1:3]) if pair and m == chips - 1 else lines[-1] for m in range(chips)]
        pieces.append([lines[-1]] + [flip(sends[m], "node", 2 * m, nodes) for m in range(1, chips)])
        if not pair:
            own_x, sib_x = cut(place, tokens, after(sib_tokens, lines[0]), chips, block, core)
    own_turned, sib_turned = turn(own_x, sib_x)

    def raw_of(pair, *others):
        sib, own = (after(x, *others) if others else x for x in (sib_x, own_x))
        return raw_terms(place, own, pieces[pair]), [swap(part) for part in raw_terms(place, sib, pieces[pair])]

    gks, sib_gks, sums, got = [], [], [], []
    raw, sib_raw = raw_of(0)
    for pair in range(PAIRS):
        gks.append(list(attend(pair, group, pos, cosine, sine, raw, sib_raw, queries, values, upstream)))
        sib_gks.append([swap(gk) for gk in gks[-1]])
        outs = list(terms(locs, place, own_turned, sib_turned, gks[-1], sib_gks[-1]))
        if pair + 1 < PAIRS:
            raw, sib_raw = raw_of(pair + 1, outs[0])
        sends = [after(out, *parts[1:]) if pair and m == chips - 1 else out for m, out in enumerate(outs)]
        parts = outs[:1] + [flip(sends[m], "node", 2 * m, nodes) for m in range(1, chips)]
        if pair + 1 == PAIRS:
            theirs, mine = (
                back(place, [[after(group[0], outs[0])] + group[1:] for group in grads], pieces, block, 1)[0]
                for grads in (sib_gks, gks)
            )
            parts[0] = after(parts[0], theirs, mine, *got[-1])
        sums.append(add(locs, place, parts, [part[1] for part in sums]))
        got.append([flip(sums[-1][k], "local", k, locs) for k in range(2, locs)])

    beside = flip(sums[-1][1], "local", 1, locs)
    grad_tokens = join(place, [mine], [swap(after(theirs, sums[-1][0]))], core)
    wholes = []
    for pair, parts in enumerate(got):
        whole = after(sums[pair][0], grad_tokens)
        for part in [beside[:, pair * width : (pair + 1) * width]] + parts:
            whole = whole + part.astype(jnp.float32)
        wholes.append(whole)
    return grad_tokens, jnp.concatenate(wholes, axis=1)


def solution(mesh):
    split = P(("node", "local"), None)
    return jax.shard_map(
        per_device,
        mesh=mesh,
        in_specs=(split, split, split, split, split, P(("node", "local"))),
        out_specs=(split, split),
        check_vma=False,
    )
```

```python
import functools
import math

import jax
import jax.numpy as jnp
from jax import lax
from jax.experimental import pallas as pl
from jax.experimental.pallas import tpu as pltpu
from jax.sharding import PartitionSpec as P

HEAD_SIZE = 128
PAIRS = 2
BATCH = 4
HBM = pl.BlockSpec(memory_space=pltpu.HBM)
VMEM = pl.BlockSpec(memory_space=pltpu.VMEM)
SMEM = pl.BlockSpec(memory_space=pltpu.SMEM)
LAST_LAST = (((1,), (1,)), ((), ()))
MIB = 1 << 20
CHEAP = pl.CostEstimate(flops=1, bytes_accessed=1, transcendentals=0)
PARAMS = pltpu.CompilerParams(vmem_limit_bytes=12 * MIB)


def angle_tables(positions):
    half = HEAD_SIZE // 2
    freq = jnp.exp(
        -(jnp.arange(half, dtype=jnp.float32) * 2.0 / HEAD_SIZE) * jnp.log(jnp.float32(1000000.0))
    )
    angle = positions.astype(jnp.float32)[:, None] * freq[None, :]
    cosine, sine = jnp.cos(angle), jnp.sin(angle)
    return jnp.concatenate([cosine, cosine], axis=1), jnp.concatenate([-sine, sine], axis=1)


def flip(x, axis, mask, size):
    return lax.ppermute(x, axis, [(i, i ^ mask) for i in range(size)])


def line_kernel(pair, place_ref, *refs):
    shards, out_ref = refs[:-1], refs[-1]
    width = out_ref.shape[2]
    for k, shard in enumerate(shards):
        first = pair * width if shard.shape[1] > width else 0
        out_ref[place_ref[1] ^ k] = shard[:, first : first + width]


def put_in_line(pair, width, place, shards):
    return pl.pallas_call(
        functools.partial(line_kernel, pair),
        out_shape=jax.ShapeDtypeStruct((len(shards), shards[0].shape[0], width), shards[0].dtype),
        in_specs=[SMEM] + [VMEM] * len(shards),
        out_specs=VMEM,
        compiler_params=PARAMS,
        cost_estimate=CHEAP,
        name="line",
    )(place, *shards)


def turn_kernel(*refs):
    half = len(refs) // 2
    for x_ref, out_ref in zip(refs[:half], refs[half:]):
        for chip in range(x_ref.shape[0]):
            out_ref[chip] = x_ref[chip].T


def turn(*arrays):
    chips, count, block = arrays[0].shape
    return pl.pallas_call(
        turn_kernel,
        out_shape=[jax.ShapeDtypeStruct((chips, block, count), arrays[0].dtype)] * len(arrays),
        in_specs=[VMEM] * len(arrays),
        out_specs=[VMEM] * len(arrays),
        compiler_params=PARAMS,
        cost_estimate=CHEAP,
        name="turn",
    )(*arrays)


def raw_kernel(place_ref, x_ref, *refs):
    pieces, outs = refs[: x_ref.shape[0]], refs[x_ref.shape[0] :]
    chip = place_ref[0] // 2
    total = jnp.zeros((x_ref.shape[1], pieces[0].shape[2]), jnp.float32)
    for m, piece in enumerate(pieces):
        locs, rows, width = piece.shape
        total += jnp.dot(
            x_ref[chip ^ m], piece[...].reshape(locs * rows, width), preferred_element_type=jnp.float32
        )
    width = outs[0].shape[1]
    for n, out_ref in enumerate(outs):
        out_ref[...] = total[:, n * width : (n + 1) * width]


def raw_terms(place, x, pieces):
    chips, count, block = x.shape
    width = pieces[0].shape[2]
    return pl.pallas_call(
        raw_kernel,
        out_shape=[jax.ShapeDtypeStruct((count, HEAD_SIZE), jnp.float32)] * (width // HEAD_SIZE),
        in_specs=[SMEM] + [VMEM] * (1 + len(pieces)),
        out_specs=[VMEM] * (width // HEAD_SIZE),
        compiler_params=PARAMS,
        cost_estimate=CHEAP,
        name="raw",
    )(place, x, *pieces)


def attend_kernel(pair, heads, group, pos_ref, cos_ref, sin_ref, *refs):
    raws, sib_raws, (q, v, u), outs = refs[:heads], refs[heads : 2 * heads], refs[2 * heads : 2 * heads + 3], refs[-heads:]
    width = heads * HEAD_SIZE
    count = outs[0].shape[0]
    block = count // 2
    biases = []
    for part in range(2):
        span = block * (part + 1)
        j = lax.broadcasted_iota(jnp.int32, (span, block), 0)
        i = lax.broadcasted_iota(jnp.int32, (span, block), 1) + part * block
        low = i - pos_ref[:, part * block : (part + 1) * block]
        biases.append(jnp.where((j <= i) & (j >= low), jnp.float32(0.0), jnp.float32(-1e30)))
    cosine, sine = cos_ref[...], sin_ref[...]
    scale = HEAD_SIZE ** (-0.5)
    slope = scale * math.log2(math.e)
    for head in range(heads):
        mine = raws[head][...] + sib_raws[head][...]
        keys = (mine * cosine + pltpu.roll(mine, HEAD_SIZE // 2, 1) * sine).astype(jnp.bfloat16)
        vals = v[:, pair * width + head * HEAD_SIZE : pair * width + (head + 1) * HEAD_SIZE]
        totals = []
        for part in range(2):
            span = block * (part + 1)
            lines = slice(part * block, (part + 1) * block)
            bias = jnp.concatenate([biases[part]] * BATCH, axis=1)
            total = jnp.zeros((span, HEAD_SIZE), jnp.float32)
            for g in range(0, group, BATCH):
                starts = [((pair * heads + head) * group + g + t) * HEAD_SIZE for t in range(BATCH)]
                at = [slice(start, start + HEAD_SIZE) for start in starts]
                qs = jnp.concatenate([q[lines, a] for a in at], axis=0)
                us = jnp.concatenate([u[lines, a] for a in at], axis=0)
                scores = lax.dot_general(keys[:span], qs, LAST_LAST, preferred_element_type=jnp.float32) + bias
                slopes = lax.dot_general(vals[:span], us, LAST_LAST, preferred_element_type=jnp.float32)
                top = jnp.max(scores, axis=0, keepdims=True)
                expo = jnp.exp2((scores - top) * slope)
                inv = 1.0 / jnp.sum(expo, axis=0, keepdims=True)
                inner = jnp.sum(expo * slopes, axis=0, keepdims=True) * inv
                dscores = (expo * (slopes - inner) * (inv * scale)).astype(jnp.bfloat16)
                total += jnp.dot(dscores, qs, preferred_element_type=jnp.float32)
            totals.append(total)
        drot = jnp.concatenate([totals[0] + totals[1][:block], totals[1][block:]], axis=0)
        outs[head][...] = (drot * cosine - pltpu.roll(drot, HEAD_SIZE // 2, 1) * sine).astype(jnp.bfloat16)


def attend(pair, group, pos, cosine, sine, raw, sib_raw, q, v, u):
    heads, (count, width) = len(raw), raw[0].shape
    q, v, u = (pltpu.with_memory_space_constraint(x, pltpu.VMEM) for x in (q, v, u))
    return pl.pallas_call(
        functools.partial(attend_kernel, pair, heads, group),
        out_shape=[jax.ShapeDtypeStruct((count, width), jnp.bfloat16)] * heads,
        in_specs=[VMEM] * (6 + 2 * heads),
        out_specs=[VMEM] * heads,
        compiler_params=PARAMS,
        cost_estimate=CHEAP,
        name="attend",
    )(pos, cosine, sine, *raw, *sib_raw, q, v, u)


def terms_kernel(heads, place_ref, own_ref, sib_ref, *refs):
    outs = refs[2 * heads :]
    chip = place_ref[0] // 2
    gk, sib_gk = (jnp.concatenate([ref[...] for ref in refs[n : n + heads]], axis=1) for n in (0, heads))

    def term(m, dtype):
        total = jnp.dot(own_ref[chip ^ m], gk, preferred_element_type=jnp.float32)
        total += jnp.dot(sib_ref[chip ^ m], sib_gk, preferred_element_type=jnp.float32)
        return total.reshape(outs[0].shape).astype(dtype)

    for m in list(range(1, len(outs))) + [0]:
        outs[m][...] = term(m, outs[m].dtype)


def terms(locs, place, own, sib, gk, sib_gk):
    chips, block, count = own.shape
    heads, width = len(gk), len(gk) * gk[0].shape[1]
    outs = [
        jax.ShapeDtypeStruct((locs, block // locs, width), jnp.bfloat16 if m else jnp.float32) for m in range(chips)
    ]
    return pl.pallas_call(
        functools.partial(terms_kernel, heads),
        out_shape=outs,
        in_specs=[SMEM] + [VMEM] * (2 + 2 * heads),
        out_specs=[VMEM] * len(outs),
        compiler_params=PARAMS,
        cost_estimate=CHEAP,
        name="terms",
    )(place, own, sib, *gk, *sib_gk)


def add_kernel(locs, count, place_ref, *refs):
    parts, earlier, outs = refs[:count], refs[count:-locs], refs[-locs:]
    width = outs[0].shape[1]
    for k in range(locs):
        total = parts[0][place_ref[1] ^ k]
        for part in parts[1:]:
            total += part[place_ref[1] ^ k].astype(jnp.float32)
        if k == 1:
            for n, ref in enumerate(earlier):
                outs[k][:, n * width : (n + 1) * width] = ref[...]
            outs[k][:, len(earlier) * width :] = total.astype(jnp.bfloat16)
        else:
            outs[k][...] = total.astype(outs[k].dtype)


def add(locs, place, parts, earlier):
    rows, width = parts[0].shape[1:]
    outs = [jax.ShapeDtypeStruct((rows, width), jnp.bfloat16 if k else jnp.float32) for k in range(locs)]
    outs[1] = jax.ShapeDtypeStruct((rows, (len(earlier) + 1) * width), jnp.bfloat16)
    return pl.pallas_call(
        functools.partial(add_kernel, locs, len(parts)),
        out_shape=outs,
        in_specs=[SMEM] + [VMEM] * (len(parts) + len(earlier)),
        out_specs=[VMEM] * locs,
        compiler_params=PARAMS,
        cost_estimate=CHEAP,
        name="add",
    )(place, *parts, *earlier)


def back_kernel(pairs, heads, parts, place_ref, *refs):
    pieces, outs = refs[pairs * heads : len(refs) - parts], refs[len(refs) - parts :]
    grads = [
        jnp.concatenate([ref[...] for ref in refs[pair * heads : (pair + 1) * heads]], axis=1) for pair in range(pairs)
    ]
    chips = len(pieces) // pairs
    for m in range(chips):
        total = None
        for pair in range(pairs):
            piece = pieces[pair * chips + m]
            locs, rows, width = piece.shape
            term = lax.dot_general(
                grads[pair], piece[...].reshape(locs * rows, width), LAST_LAST, preferred_element_type=jnp.float32
            )
            total = term if total is None else total + term
        outs[m * parts // chips][m % (chips // parts)] = total.astype(jnp.bfloat16)


def back(place, gks, pieces, block, parts):
    pairs, heads, chips = len(pieces), len(gks[0]), len(pieces[0])
    return pl.pallas_call(
        functools.partial(back_kernel, pairs, heads, parts),
        out_shape=[jax.ShapeDtypeStruct((chips // parts, gks[0][0].shape[0], block), jnp.bfloat16)] * parts,
        in_specs=[SMEM] + [VMEM] * (pairs * heads + pairs * chips),
        out_specs=[VMEM] * parts,
        compiler_params=PARAMS,
        cost_estimate=CHEAP,
        name="back",
    )(place, *[gk for group in gks for gk in group], *[piece for group in pieces for piece in group])


def columns_of(array, chip, core, block):
    return array.at[:, pl.ds(pl.multiple_of((2 * chip + core) * block, block), block)]


def cut_kernel(place_ref, x_hbm, sib_hbm, own_ref, sib_ref, sems):
    core = place_ref[0] & 1
    copies = []
    for chip in range(own_ref.shape[0]):
        for n, (array, out_ref) in enumerate(((x_hbm, own_ref), (sib_hbm, sib_ref))):
            source = columns_of(array, chip, core, own_ref.shape[2])
            copies.append(pltpu.make_async_copy(source, out_ref.at[chip], sems.at[2 * chip + n]))
    for copy in copies:
        copy.start()
    for copy in copies:
        copy.wait()


def cut(place, x, sib_x, chips, block, core):
    count = x.shape[0]
    if block % 128:
        blocks = [array.reshape(count, chips, 2, block).transpose(2, 1, 0, 3) for array in (x, sib_x)]
        return [lax.dynamic_index_in_dim(array, core, axis=0, keepdims=False) for array in blocks]
    return pl.pallas_call(
        cut_kernel,
        out_shape=[jax.ShapeDtypeStruct((chips, count, block), x.dtype)] * 2,
        in_specs=[SMEM, HBM, pl.BlockSpec(memory_space=pl.ANY)],
        out_specs=[VMEM] * 2,
        scratch_shapes=[pltpu.SemaphoreType.DMA((2 * chips,))],
        compiler_params=PARAMS,
        cost_estimate=CHEAP,
        name="cut",
    )(place, pin(x), sib_x)


def join_kernel(place_ref, *refs):
    parts, out_hbm, sems = refs[:-2], refs[-2], refs[-1]
    chip, core = place_ref[0] // 2, place_ref[0] & 1
    block = parts[0].shape[2]
    copies = []
    for n, same in enumerate((parts[:1], parts[1:])):
        m = 0
        for part in same:
            for i in range(part.shape[0]):
                target = columns_of(out_hbm, chip ^ m, core ^ n, block)
                copies.append(pltpu.make_async_copy(part.at[i], target, sems.at[2 * m + n]))
                m += 1
    for copy in copies:
        copy.start()
    for copy in copies:
        copy.wait()


def join(place, own, sib, core):
    (own,) = own
    chips, count, block = own.shape
    if block % 128:
        sib = jnp.concatenate(sib)
        both = jnp.where(core == 0, jnp.stack([own, sib]), jnp.stack([sib, own]))
        both = jnp.take(both, jnp.arange(chips) ^ (place[0] // 2), axis=1)
        return both.transpose(2, 1, 0, 3).reshape(count, 2 * chips * block)
    return pl.pallas_call(
        join_kernel,
        out_shape=jax.ShapeDtypeStruct((count, 2 * chips * block), own.dtype),
        in_specs=[SMEM] + [VMEM] * (1 + len(sib)),
        out_specs=HBM,
        scratch_shapes=[pltpu.SemaphoreType.DMA((2 * chips,))],
        compiler_params=PARAMS,
        cost_estimate=CHEAP,
        name="join",
    )(place, own, *sib)


def pin(x):
    return pltpu.with_memory_space_constraint(x, pltpu.HBM)


def after(x, *others):
    return lax.optimization_barrier((x, *others))[0]


def per_device(tokens, queries, values, upstream, key_weight, positions):
    nodes, locs = lax.axis_size("node"), lax.axis_size("local")
    chips = nodes // 2
    key_width = key_weight.shape[1]
    count, model = tokens.shape
    block = model // nodes
    group = queries.shape[1] // key_width
    width = key_width // PAIRS
    node, local = lax.axis_index("node"), lax.axis_index("local")
    core = node & 1
    place = jnp.stack([node, local]).astype(jnp.int32)

    def swap(x):
        return flip(x, "node", 1, nodes)

    sib_tokens = swap(tokens)
    cosine, sine = angle_tables(positions)
    pos = positions.reshape(1, count)
    lines, pieces = [], []
    beside = flip(key_weight, "local", 1, locs)
    for pair in range(PAIRS):
        own = key_weight[:, pair * width : (pair + 1) * width]
        if pair:
            own = after(own, lines[-1])
        shards = [own, beside] + [flip(own, "local", k, locs) for k in range(2, locs)]
        shards[-1] = after(shards[-1], *((own_x, pieces[-1][-1]) if pair else (sib_tokens, cosine, sine)))
        lines.append(put_in_line(pair, width, place, shards))
        sends = [after(lines[-1], *pieces[-1][1:3]) if pair and m == chips - 1 else lines[-1] for m in range(chips)]
        pieces.append([lines[-1]] + [flip(sends[m], "node", 2 * m, nodes) for m in range(1, chips)])
        if not pair:
            own_x, sib_x = cut(place, tokens, after(sib_tokens, lines[0]), chips, block, core)
    own_turned, sib_turned = turn(own_x, sib_x)

    def raw_of(pair, *others):
        sib, own = (after(x, *others) if others else x for x in (sib_x, own_x))
        return raw_terms(place, own, pieces[pair]), [swap(part) for part in raw_terms(place, sib, pieces[pair])]

    gks, sib_gks, sums, got = [], [], [], []
    raw, sib_raw = raw_of(0)
    for pair in range(PAIRS):
        gks.append(list(attend(pair, group, pos, cosine, sine, raw, sib_raw, queries, values, upstream)))
        sib_gks.append([swap(gk) for gk in gks[-1]])
        outs = list(terms(locs, place, own_turned, sib_turned, gks[-1], sib_gks[-1]))
        if pair + 1 < PAIRS:
            raw, sib_raw = raw_of(pair + 1, outs[0])
        sends = [after(out, *parts[1:]) if pair and m == 1 else out for m, out in enumerate(outs)]
        parts = outs[:1] + [flip(sends[m], "node", 2 * m, nodes) for m in range(1, chips)]
        if pair + 1 == PAIRS:
            theirs, mine = (
                back(place, [[after(group[0], outs[0])] + group[1:] for group in grads], pieces, block, 1)[0]
                for grads in (sib_gks, gks)
            )
            parts[0] = after(parts[0], theirs, mine, *got[-1])
        sums.append(add(locs, place, parts, [part[1] for part in sums]))
        got.append([flip(sums[-1][k], "local", k, locs) for k in range(2, locs)])

    beside = flip(sums[-1][1], "local", 1, locs)
    grad_tokens = join(place, [mine], [swap(after(theirs, sums[-1][0]))], core)
    wholes = []
    for pair, parts in enumerate(got):
        whole = after(sums[pair][0], grad_tokens)
        for part in [beside[:, pair * width : (pair + 1) * width]] + parts:
            whole = whole + part.astype(jnp.float32)
        wholes.append(whole)
    return grad_tokens, jnp.concatenate(wholes, axis=1)


def solution(mesh):
    split = P(("node", "local"), None)
    return jax.shard_map(
        per_device,
        mesh=mesh,
        in_specs=(split, split, split, split, split, P(("node", "local"))),
        out_specs=(split, split),
        check_vma=False,
    )
```

```python
import functools
import math

import jax
import jax.numpy as jnp
from jax import lax
from jax.experimental import pallas as pl
from jax.experimental.pallas import tpu as pltpu
from jax.sharding import PartitionSpec as P

HEAD_SIZE = 128
PAIRS = 2
BATCH = 8
HBM = pl.BlockSpec(memory_space=pltpu.HBM)
VMEM = pl.BlockSpec(memory_space=pltpu.VMEM)
SMEM = pl.BlockSpec(memory_space=pltpu.SMEM)
LAST_LAST = (((1,), (1,)), ((), ()))
MIB = 1 << 20
CHEAP = pl.CostEstimate(flops=1, bytes_accessed=1, transcendentals=0)
PARAMS = pltpu.CompilerParams(vmem_limit_bytes=12 * MIB)


def angle_tables(positions):
    half = HEAD_SIZE // 2
    freq = jnp.exp(
        -(jnp.arange(half, dtype=jnp.float32) * 2.0 / HEAD_SIZE) * jnp.log(jnp.float32(1000000.0))
    )
    angle = positions.astype(jnp.float32)[:, None] * freq[None, :]
    cosine, sine = jnp.cos(angle), jnp.sin(angle)
    return jnp.concatenate([cosine, cosine], axis=1), jnp.concatenate([-sine, sine], axis=1)


def flip(x, axis, mask, size):
    return lax.ppermute(x, axis, [(i, i ^ mask) for i in range(size)])


def line_kernel(pair, place_ref, *refs):
    shards, out_ref = refs[:-1], refs[-1]
    width = out_ref.shape[2]
    for k, shard in enumerate(shards):
        first = pair * width if shard.shape[1] > width else 0
        out_ref[place_ref[1] ^ k] = shard[:, first : first + width]


def put_in_line(pair, width, place, shards):
    return pl.pallas_call(
        functools.partial(line_kernel, pair),
        out_shape=jax.ShapeDtypeStruct((len(shards), shards[0].shape[0], width), shards[0].dtype),
        in_specs=[SMEM] + [VMEM] * len(shards),
        out_specs=VMEM,
        compiler_params=PARAMS,
        cost_estimate=CHEAP,
        name="line",
    )(place, *shards)


def turn_kernel(*refs):
    half = len(refs) // 2
    for x_ref, out_ref in zip(refs[:half], refs[half:]):
        for chip in range(x_ref.shape[0]):
            out_ref[chip] = x_ref[chip].T


def turn(*arrays):
    chips, count, block = arrays[0].shape
    return pl.pallas_call(
        turn_kernel,
        out_shape=[jax.ShapeDtypeStruct((chips, block, count), arrays[0].dtype)] * len(arrays),
        in_specs=[VMEM] * len(arrays),
        out_specs=[VMEM] * len(arrays),
        compiler_params=PARAMS,
        cost_estimate=CHEAP,
        name="turn",
    )(*arrays)


def raw_kernel(place_ref, x_ref, *refs):
    pieces, outs = refs[: x_ref.shape[0]], refs[x_ref.shape[0] :]
    chip = place_ref[0] // 2
    total = jnp.zeros((x_ref.shape[1], pieces[0].shape[2]), jnp.float32)
    for m, piece in enumerate(pieces):
        locs, rows, width = piece.shape
        total += jnp.dot(
            x_ref[chip ^ m], piece[...].reshape(locs * rows, width), preferred_element_type=jnp.float32
        )
    width = outs[0].shape[1]
    for n, out_ref in enumerate(outs):
        out_ref[...] = total[:, n * width : (n + 1) * width]


def raw_terms(place, x, pieces):
    chips, count, block = x.shape
    width = pieces[0].shape[2]
    return pl.pallas_call(
        raw_kernel,
        out_shape=[jax.ShapeDtypeStruct((count, HEAD_SIZE), jnp.float32)] * (width // HEAD_SIZE),
        in_specs=[SMEM] + [VMEM] * (1 + len(pieces)),
        out_specs=[VMEM] * (width // HEAD_SIZE),
        compiler_params=PARAMS,
        cost_estimate=CHEAP,
        name="raw",
    )(place, x, *pieces)


def attend_kernel(pair, heads, group, pos_ref, cos_ref, sin_ref, *refs):
    raws, sib_raws, (q, v, u), outs = refs[:heads], refs[heads : 2 * heads], refs[2 * heads : 2 * heads + 3], refs[-heads:]
    width = heads * HEAD_SIZE
    count = outs[0].shape[0]
    block = count // 2
    biases = []
    for part in range(2):
        span = block * (part + 1)
        j = lax.broadcasted_iota(jnp.int32, (span, block), 0)
        i = lax.broadcasted_iota(jnp.int32, (span, block), 1) + part * block
        low = i - pos_ref[:, part * block : (part + 1) * block]
        biases.append(jnp.where((j <= i) & (j >= low), jnp.float32(0.0), jnp.float32(-1e30)))
    cosine, sine = cos_ref[...], sin_ref[...]
    scale = HEAD_SIZE ** (-0.5)
    slope = scale * math.log2(math.e)
    for head in range(heads):
        mine = raws[head][...] + sib_raws[head][...]
        keys = (mine * cosine + pltpu.roll(mine, HEAD_SIZE // 2, 1) * sine).astype(jnp.bfloat16)
        vals = v[:, pair * width + head * HEAD_SIZE : pair * width + (head + 1) * HEAD_SIZE]
        totals = []
        for part in range(2):
            span = block * (part + 1)
            lines = slice(part * block, (part + 1) * block)
            bias = jnp.concatenate([biases[part]] * BATCH, axis=1)
            total = jnp.zeros((span, HEAD_SIZE), jnp.float32)
            for g in range(0, group, BATCH):
                starts = [((pair * heads + head) * group + g + t) * HEAD_SIZE for t in range(BATCH)]
                at = [slice(start, start + HEAD_SIZE) for start in starts]
                qs = jnp.concatenate([q[lines, a] for a in at], axis=0)
                us = jnp.concatenate([u[lines, a] for a in at], axis=0)
                scores = lax.dot_general(keys[:span], qs, LAST_LAST, preferred_element_type=jnp.float32) + bias
                slopes = lax.dot_general(vals[:span], us, LAST_LAST, preferred_element_type=jnp.float32)
                top = jnp.max(scores, axis=0, keepdims=True)
                expo = jnp.exp2((scores - top) * slope)
                inv = 1.0 / jnp.sum(expo, axis=0, keepdims=True)
                inner = jnp.sum(expo * slopes, axis=0, keepdims=True) * inv
                dscores = (expo * (slopes - inner) * (inv * scale)).astype(jnp.bfloat16)
                total += jnp.dot(dscores, qs, preferred_element_type=jnp.float32)
            totals.append(total)
        drot = jnp.concatenate([totals[0] + totals[1][:block], totals[1][block:]], axis=0)
        outs[head][...] = (drot * cosine - pltpu.roll(drot, HEAD_SIZE // 2, 1) * sine).astype(jnp.bfloat16)


def attend(pair, group, pos, cosine, sine, raw, sib_raw, q, v, u):
    heads, (count, width) = len(raw), raw[0].shape
    q, v, u = (pltpu.with_memory_space_constraint(x, pltpu.VMEM) for x in (q, v, u))
    return pl.pallas_call(
        functools.partial(attend_kernel, pair, heads, group),
        out_shape=[jax.ShapeDtypeStruct((count, width), jnp.bfloat16)] * heads,
        in_specs=[VMEM] * (6 + 2 * heads),
        out_specs=[VMEM] * heads,
        compiler_params=PARAMS,
        cost_estimate=CHEAP,
        name="attend",
    )(pos, cosine, sine, *raw, *sib_raw, q, v, u)


def terms_kernel(heads, place_ref, own_ref, sib_ref, *refs):
    outs = refs[2 * heads :]
    chip = place_ref[0] // 2
    gk, sib_gk = (jnp.concatenate([ref[...] for ref in refs[n : n + heads]], axis=1) for n in (0, heads))

    def term(m, dtype):
        total = jnp.dot(own_ref[chip ^ m], gk, preferred_element_type=jnp.float32)
        total += jnp.dot(sib_ref[chip ^ m], sib_gk, preferred_element_type=jnp.float32)
        return total.reshape(outs[0].shape).astype(dtype)

    for m in list(range(1, len(outs))) + [0]:
        outs[m][...] = term(m, outs[m].dtype)


def terms(locs, place, own, sib, gk, sib_gk):
    chips, block, count = own.shape
    heads, width = len(gk), len(gk) * gk[0].shape[1]
    outs = [
        jax.ShapeDtypeStruct((locs, block // locs, width), jnp.bfloat16 if m else jnp.float32) for m in range(chips)
    ]
    return pl.pallas_call(
        functools.partial(terms_kernel, heads),
        out_shape=outs,
        in_specs=[SMEM] + [VMEM] * (2 + 2 * heads),
        out_specs=[VMEM] * len(outs),
        compiler_params=PARAMS,
        cost_estimate=CHEAP,
        name="terms",
    )(place, own, sib, *gk, *sib_gk)


def add_kernel(locs, count, place_ref, *refs):
    parts, earlier, outs = refs[:count], refs[count:-locs], refs[-locs:]
    width = outs[0].shape[1]
    for k in range(locs):
        total = parts[0][place_ref[1] ^ k]
        for part in parts[1:]:
            total += part[place_ref[1] ^ k].astype(jnp.float32)
        if k == 1:
            for n, ref in enumerate(earlier):
                outs[k][:, n * width : (n + 1) * width] = ref[...]
            outs[k][:, len(earlier) * width :] = total.astype(jnp.bfloat16)
        else:
            outs[k][...] = total.astype(outs[k].dtype)


def add(locs, place, parts, earlier):
    rows, width = parts[0].shape[1:]
    outs = [jax.ShapeDtypeStruct((rows, width), jnp.bfloat16 if k else jnp.float32) for k in range(locs)]
    outs[1] = jax.ShapeDtypeStruct((rows, (len(earlier) + 1) * width), jnp.bfloat16)
    return pl.pallas_call(
        functools.partial(add_kernel, locs, len(parts)),
        out_shape=outs,
        in_specs=[SMEM] + [VMEM] * (len(parts) + len(earlier)),
        out_specs=[VMEM] * locs,
        compiler_params=PARAMS,
        cost_estimate=CHEAP,
        name="add",
    )(place, *parts, *earlier)


def back_kernel(pairs, heads, parts, place_ref, *refs):
    pieces, outs = refs[pairs * heads : len(refs) - parts], refs[len(refs) - parts :]
    grads = [
        jnp.concatenate([ref[...] for ref in refs[pair * heads : (pair + 1) * heads]], axis=1) for pair in range(pairs)
    ]
    chips = len(pieces) // pairs
    for m in range(chips):
        total = None
        for pair in range(pairs):
            piece = pieces[pair * chips + m]
            locs, rows, width = piece.shape
            term = lax.dot_general(
                grads[pair], piece[...].reshape(locs * rows, width), LAST_LAST, preferred_element_type=jnp.float32
            )
            total = term if total is None else total + term
        outs[m * parts // chips][m % (chips // parts)] = total.astype(jnp.bfloat16)


def back(place, gks, pieces, block, parts):
    pairs, heads, chips = len(pieces), len(gks[0]), len(pieces[0])
    return pl.pallas_call(
        functools.partial(back_kernel, pairs, heads, parts),
        out_shape=[jax.ShapeDtypeStruct((chips // parts, gks[0][0].shape[0], block), jnp.bfloat16)] * parts,
        in_specs=[SMEM] + [VMEM] * (pairs * heads + pairs * chips),
        out_specs=[VMEM] * parts,
        compiler_params=PARAMS,
        cost_estimate=CHEAP,
        name="back",
    )(place, *[gk for group in gks for gk in group], *[piece for group in pieces for piece in group])


def columns_of(array, chip, core, block):
    return array.at[:, pl.ds(pl.multiple_of((2 * chip + core) * block, block), block)]


def cut_kernel(place_ref, x_hbm, sib_hbm, own_ref, sib_ref, sems):
    core = place_ref[0] & 1
    copies = []
    for chip in range(own_ref.shape[0]):
        for n, (array, out_ref) in enumerate(((x_hbm, own_ref), (sib_hbm, sib_ref))):
            source = columns_of(array, chip, core, own_ref.shape[2])
            copies.append(pltpu.make_async_copy(source, out_ref.at[chip], sems.at[2 * chip + n]))
    for copy in copies:
        copy.start()
    for copy in copies:
        copy.wait()


def cut(place, x, sib_x, chips, block, core):
    count = x.shape[0]
    if block % 128:
        blocks = [array.reshape(count, chips, 2, block).transpose(2, 1, 0, 3) for array in (x, sib_x)]
        return [lax.dynamic_index_in_dim(array, core, axis=0, keepdims=False) for array in blocks]
    return pl.pallas_call(
        cut_kernel,
        out_shape=[jax.ShapeDtypeStruct((chips, count, block), x.dtype)] * 2,
        in_specs=[SMEM, HBM, pl.BlockSpec(memory_space=pl.ANY)],
        out_specs=[VMEM] * 2,
        scratch_shapes=[pltpu.SemaphoreType.DMA((2 * chips,))],
        compiler_params=PARAMS,
        cost_estimate=CHEAP,
        name="cut",
    )(place, pin(x), sib_x)


def join_kernel(place_ref, *refs):
    parts, out_hbm, sems = refs[:-2], refs[-2], refs[-1]
    chip, core = place_ref[0] // 2, place_ref[0] & 1
    block = parts[0].shape[2]
    copies = []
    for n, same in enumerate((parts[:1], parts[1:])):
        m = 0
        for part in same:
            for i in range(part.shape[0]):
                target = columns_of(out_hbm, chip ^ m, core ^ n, block)
                copies.append(pltpu.make_async_copy(part.at[i], target, sems.at[2 * m + n]))
                m += 1
    for copy in copies:
        copy.start()
    for copy in copies:
        copy.wait()


def join(place, own, sib, core):
    (own,) = own
    chips, count, block = own.shape
    if block % 128:
        sib = jnp.concatenate(sib)
        both = jnp.where(core == 0, jnp.stack([own, sib]), jnp.stack([sib, own]))
        both = jnp.take(both, jnp.arange(chips) ^ (place[0] // 2), axis=1)
        return both.transpose(2, 1, 0, 3).reshape(count, 2 * chips * block)
    return pl.pallas_call(
        join_kernel,
        out_shape=jax.ShapeDtypeStruct((count, 2 * chips * block), own.dtype),
        in_specs=[SMEM] + [VMEM] * (1 + len(sib)),
        out_specs=HBM,
        scratch_shapes=[pltpu.SemaphoreType.DMA((2 * chips,))],
        compiler_params=PARAMS,
        cost_estimate=CHEAP,
        name="join",
    )(place, own, *sib)


def pin(x):
    return pltpu.with_memory_space_constraint(x, pltpu.HBM)


def after(x, *others):
    return lax.optimization_barrier((x, *others))[0]


def per_device(tokens, queries, values, upstream, key_weight, positions):
    nodes, locs = lax.axis_size("node"), lax.axis_size("local")
    chips = nodes // 2
    key_width = key_weight.shape[1]
    count, model = tokens.shape
    block = model // nodes
    group = queries.shape[1] // key_width
    width = key_width // PAIRS
    node, local = lax.axis_index("node"), lax.axis_index("local")
    core = node & 1
    place = jnp.stack([node, local]).astype(jnp.int32)

    def swap(x):
        return flip(x, "node", 1, nodes)

    sib_tokens = swap(tokens)
    lines, pieces = [], []
    beside = flip(key_weight, "local", 1, locs)
    for pair in range(PAIRS):
        own = key_weight[:, pair * width : (pair + 1) * width]
        if pair:
            own = after(own, lines[-1])
        shards = [own, beside] + [flip(own, "local", k, locs) for k in range(2, locs)]
        shards[-1] = after(shards[-1], *((own_x, pieces[-1][-1]) if pair else (sib_tokens,)))
        lines.append(put_in_line(pair, width, place, shards))
        pieces.append([lines[-1]] + [flip(lines[-1], "node", 2 * m, nodes) for m in range(1, chips)])
        if not pair:
            own_x, sib_x = cut(place, tokens, after(sib_tokens, lines[0]), chips, block, core)
    own_turned, sib_turned = turn(own_x, sib_x)

    cosine, sine = angle_tables(positions)
    pos = positions.reshape(1, count)

    def raw_of(pair, *others):
        sib, own = (after(x, *others) if others else x for x in (sib_x, own_x))
        return raw_terms(place, own, pieces[pair]), [swap(part) for part in raw_terms(place, sib, pieces[pair])]

    gks, sib_gks, sums, got = [], [], [], []
    raw, sib_raw = raw_of(0)
    for pair in range(PAIRS):
        gks.append(list(attend(pair, group, pos, cosine, sine, raw, sib_raw, queries, values, upstream)))
        sib_gks.append([swap(gk) for gk in gks[-1]])
        outs = list(terms(locs, place, own_turned, sib_turned, gks[-1], sib_gks[-1]))
        if pair + 1 < PAIRS:
            raw, sib_raw = raw_of(pair + 1, outs[0])
        sends = [after(out, *parts[1:]) if pair and m == chips - 1 else out for m, out in enumerate(outs)]
        parts = outs[:1] + [flip(sends[m], "node", 2 * m, nodes) for m in range(1, chips)]
        if pair + 1 == PAIRS:
            theirs, mine = (
                back(place, [[after(group[0], outs[0])] + group[1:] for group in grads], pieces, block, 1)[0]
                for grads in (sib_gks, gks)
            )
            parts[0] = after(parts[0], theirs, mine, *got[-1])
        sums.append(add(locs, place, parts, [part[1] for part in sums]))
        got.append([flip(sums[-1][k], "local", k, locs) for k in range(2, locs)])

    beside = flip(sums[-1][1], "local", 1, locs)
    grad_tokens = join(place, [mine], [swap(after(theirs, sums[-1][0]))], core)
    wholes = []
    for pair, parts in enumerate(got):
        whole = after(sums[pair][0], grad_tokens)
        for part in [beside[:, pair * width : (pair + 1) * width]] + parts:
            whole = whole + part.astype(jnp.float32)
        wholes.append(whole)
    return grad_tokens, jnp.concatenate(wholes, axis=1)


def solution(mesh):
    split = P(("node", "local"), None)
    return jax.shard_map(
        per_device,
        mesh=mesh,
        in_specs=(split, split, split, split, split, P(("node", "local"))),
        out_specs=(split, split),
        check_vma=False,
    )
```
